32 devices in a mesh: groups: 2 (over x), tensor: 16 (over z, y, core).
Axes of the slice: x: 2, y: 2, z: 4, core: 2. Of those that a mesh axis runs over, the one named last changes fastest.
Arguments:
- encoded_query_rows: bfloat16 [256, 16384], P('groups', 'tensor'), parts along dimension 0, may hold values from -105 to 105
- encoded_key_rows: bfloat16 [256, 1024], P(('groups', 'tensor')), parts along dimension 0, may hold values from -4 to 4
- head_value_rows: bfloat16 [256, 1024], P(('groups', 'tensor')), parts along dimension 0, may hold values from -6 to 6
- quant_codes: int32 [256, 16384], P(('groups', 'tensor')), parts along dimension 0, may hold values from -127 to 127
- exponents: int32 [256, 128], P(('groups', 'tensor')), parts along dimension 0, may hold values from -10 to -7
- out_weight: bfloat16 [16384, 16384], P('tensor'), may hold values from -0.1875 to 0.1875
Outputs:
- next_residual: bfloat16 [256, 16384], P(('groups', 'tensor')), parts along dimension 0
The draws below stay inside these ranges and needn't reach their ends.
There are 2 independent parts, one for each index of `groups`. The reference program is written for one: setup_inputs(seed, part) draws one part's arguments, and reference() takes and returns one part's arrays. A program takes and returns all parts, laid end to end along the dimension named above; an argument that names none is the same for every part. Nothing has to cross between parts.
Inputs may be any that keep to these rules, and one draw needn't show every extreme that they name: `quant_codes`: codes of the residual stream in the Hadamard-rotated basis, 128 features a block. `exponents`: one exponent for each token and block of 128 features.
All inputs are finite; a program needn't handle non-finite values.
Results may differ from the reference program's by a relative error of at most 0.0046.
Values may be sent and summed in bfloat16 or wider, within the bound.
No kernel may reach another device: no remote copies, remote signals or barrier semaphores. Data moves between devices by JAX's collectives and lax.ppermute only.
A program may use at most 128 MiB of HBM per device.

```python
import math
import jax
import jax.numpy as jnp
from jax import lax

D = 16384
QUERY_HEADS = 128
KEY_VALUE_HEADS = 8
HEAD_SIZE = 128
HBLK = 128
SEQUENCE_TOKENS = 128


def shared_keys(key):
    return jnp.clip(jax.random.normal(key, (SEQUENCE_TOKENS, KEY_VALUE_HEADS * HEAD_SIZE), jnp.float32), -4.0, 4.0)


def draw_encoded_key_rows(key, part):
    base = shared_keys(key)
    result = base
    return result.astype(jnp.bfloat16)


def draw_encoded_query_rows(key, part):
    key = jax.random.fold_in(key, 13)
    query_matrix = jnp.clip(jax.random.normal(key, (SEQUENCE_TOKENS, QUERY_HEADS * HEAD_SIZE), jnp.float32), -4.0, 4.0)
    return query_matrix.astype(jnp.bfloat16)


def set_ends(values, own_key, low, high):
    longest = values.shape.index(max(values.shape))
    spots = []
    for shift in (0, 1):
        where = [jax.random.randint(jax.random.fold_in(own_key, axis), (), 0, length) for axis, length in enumerate(values.shape)]
        where[longest] = (where[longest] + shift) % values.shape[longest]
        spots.append(tuple(where))
    return values.at[spots[0]].set(low).at[spots[1]].set(high)


def level_of(key, extent, cuts, smallest, high):
    def one(dim, blocks):
        heights = jax.random.uniform(jax.random.fold_in(jax.random.fold_in(key, 6), dim), (blocks,), jnp.float32, smallest / len(cuts), high / len(cuts))
        return jnp.repeat(jnp.exp(heights), extent[dim] // blocks).reshape((-1,) + (1,) * (len(extent) - dim - 1))

    level = one(*cuts[0])
    for cut in cuts[1:]:
        level = level * one(*cut)
    return level


def normal_values(own_key, extent, deviation, reach, cuts=(), kind=jnp.bfloat16):
    values = jax.random.normal(own_key, extent, jnp.float32) * deviation
    if len(cuts) > 0:
        values = level_of(own_key, extent, cuts, -0.22, 0.18) * values
    return jnp.clip(values, min=-reach, max=reach).astype(kind)


def setup_inputs(seed: int = 0, part: int = 0) -> dict:
    key_list = jax.random.split(jax.random.key(seed), 7)
    part_keys = jax.random.split(jax.random.fold_in(key_list[6], part), 7)
    encoded_query_rows = draw_encoded_query_rows(jax.random.fold_in(jax.random.fold_in(key_list[6], part), 71), part)
    encoded_key_rows = draw_encoded_key_rows(jax.random.fold_in(jax.random.fold_in(key_list[6], part), 71), part)
    head_value_rows = normal_values(part_keys[2], (SEQUENCE_TOKENS, KEY_VALUE_HEADS * HEAD_SIZE), 1.0, 6.0, ((0, 16),))
    quant_codes = set_ends(jax.random.randint(part_keys[3], (SEQUENCE_TOKENS, D), -127, 128), jax.random.fold_in(part_keys[3], 1), -127, 127).astype(jnp.int32)
    exponents = set_ends(jax.random.randint(part_keys[4], (SEQUENCE_TOKENS, D // HBLK), -10, -6), jax.random.fold_in(part_keys[4], 1), -10, (-6) - 1).astype(jnp.int32)
    out_weight = normal_values(key_list[5], (QUERY_HEADS * HEAD_SIZE, D), (8 * HEAD_SIZE) ** -0.5, 0.1875, ((0, 16),))
    return {"encoded_query_rows": encoded_query_rows, "encoded_key_rows": encoded_key_rows, "head_value_rows": head_value_rows, "quant_codes": quant_codes, "exponents": exponents, "out_weight": out_weight}


def hadamard_table(order):
    index = jnp.arange(order, dtype=jnp.int32)
    common = index[:, None] & index[None, :]
    parity = jnp.zeros((order, order), jnp.int32)
    for shift_bits in range(max(order.bit_length() - 1, 1)):
        parity = parity + (common >> shift_bits & 1)
    return (1 - 2 * (parity % 2)).astype(jnp.float32)

def reference(encoded_query_rows, encoded_key_rows, head_value_rows, quant_codes, exponents, out_weight):
    query_group = QUERY_HEADS // KEY_VALUE_HEADS
    scale = 1.0 / math.sqrt(HEAD_SIZE)
    query_matrix = encoded_query_rows.astype(jnp.float32).reshape(SEQUENCE_TOKENS, KEY_VALUE_HEADS, query_group, HEAD_SIZE)
    key_matrix = encoded_key_rows.astype(jnp.float32).reshape(SEQUENCE_TOKENS, KEY_VALUE_HEADS, HEAD_SIZE)
    value_matrix = head_value_rows.astype(jnp.float32).reshape(SEQUENCE_TOKENS, KEY_VALUE_HEADS, HEAD_SIZE)
    position = jnp.arange(SEQUENCE_TOKENS, dtype=jnp.int32)
    visible = position[None, :] <= position[:, None]

    def one_head(operands):
        query_block, key_block, value_block = operands
        scores = jnp.einsum('tgd,sd->gts', query_block, key_block, precision=lax.Precision.HIGHEST) * scale
        scores = jnp.where(visible[None], scores, -1e+30)
        top = lax.optimization_barrier(jnp.max(scores, axis=-1, keepdims=True))
        weights = jnp.where(visible[None], jnp.exp(scores - top), 0.0)
        total = lax.optimization_barrier(jnp.sum(weights, axis=-1, keepdims=True))
        summed = jnp.einsum('gts,sd->tgd', weights, value_block, precision=lax.Precision.HIGHEST)
        return summed / jnp.transpose(total, (1, 0, 2))
    context = lax.map(one_head, (jnp.moveaxis(query_matrix, 1, 0), jnp.moveaxis(key_matrix, 1, 0), jnp.moveaxis(value_matrix, 1, 0)))
    context = jnp.moveaxis(context, 0, 1).reshape(SEQUENCE_TOKENS, QUERY_HEADS * HEAD_SIZE).astype(jnp.bfloat16)
    projected = jnp.dot(context, out_weight, preferred_element_type=jnp.float32)
    table = hadamard_table(HBLK)
    rotated = jnp.dot(projected.reshape(-1, HBLK), table, precision=lax.Precision.HIGHEST).reshape(SEQUENCE_TOKENS, D) / math.sqrt(HBLK)
    blocks = D // HBLK
    residual = quant_codes.astype(jnp.float32).reshape(SEQUENCE_TOKENS, blocks, HBLK) * jnp.exp2(exponents.astype(jnp.float32))[:, :, None]
    return (residual.reshape(SEQUENCE_TOKENS, D) + rotated).astype(jnp.bfloat16)
```

```python
import functools
import math

import jax
import jax.numpy as jnp
from jax import lax
from jax.experimental import pallas as pl
from jax.experimental.pallas import tpu as pltpu
from jax.sharding import PartitionSpec as P

QUERY_HEADS = 128
KEY_VALUE_HEADS = 8
HEAD_SIZE = 128
HBLK = 128
masked_score = -1e30

PARTS = (4, 6, 4, 2)


def reversed_bits(index, bits):
    result = 0
    for bit in range(bits):
        result = result + ((index >> bit) & 1) * (1 << (bits - 1 - bit))
    return result


def attend(token, q_ref, kv_ref, context_ref):
    total_rows = q_ref.shape[0]
    column = lax.broadcasted_iota(jnp.int32, (total_rows, total_rows), 1)
    order = jnp.where(column == token, 1.0, 0.0).astype(jnp.bfloat16)
    visible = column <= token
    queries = jnp.dot(order, q_ref[...], preferred_element_type=jnp.float32).astype(jnp.bfloat16)
    key = kv_ref[:, :HEAD_SIZE]
    value = kv_ref[:, HEAD_SIZE:]
    for head in range(q_ref.shape[1] // HEAD_SIZE):
        columns = slice(head * HEAD_SIZE, (head + 1) * HEAD_SIZE)
        scores = lax.dot_general(
            queries[:, columns], key, (((1,), (1,)), ((), ())), preferred_element_type=jnp.float32
        ) * (1.0 / math.sqrt(HEAD_SIZE))
        scores = jnp.where(visible, scores, masked_score)
        top = jnp.max(scores, axis=1, keepdims=True)
        weights = jnp.where(visible, jnp.exp(scores - top), 0.0)
        total = jnp.sum(weights, axis=1, keepdims=True)
        high = weights.astype(jnp.bfloat16)
        low = (weights - high.astype(jnp.float32)).astype(jnp.bfloat16)
        weighted = jnp.dot(high, value, preferred_element_type=jnp.float32)
        weighted = weighted + jnp.dot(low, value, preferred_element_type=jnp.float32)
        context_ref[:, columns] = (weighted / total).astype(jnp.bfloat16)


def project(start, context_ref, w_ref, keep_ref, send_ref, buffer, arrived, prologue=None):
    tiles, _, tile = buffer.shape
    half = keep_ref.shape[0]

    def copy(index):
        return pltpu.make_async_copy(
            w_ref.at[:, pl.ds(start + index * tile, tile)], buffer.at[index], arrived.at[index]
        )

    for index in range(tiles):
        copy(index).start()
    if prologue is not None:
        prologue()
    for index in range(tiles):
        copy(index).wait()
        columns = slice(index * tile, (index + 1) * tile)
        product = jnp.dot(context_ref[...], buffer[index], preferred_element_type=jnp.float32)
        keep_ref[:, columns] = product[:half]
        send_ref[:, columns] = product[half:].astype(jnp.bfloat16)


def first_kernel(start, bits, place_ref, q_ref, kv_ref, w_ref, context_ref, keep_ref, send_ref, buffer, arrived):
    total_rows = q_ref.shape[0]
    rows = total_rows >> bits
    row = lax.broadcasted_iota(jnp.int32, (total_rows, 1), 0)
    token = (place_ref[0] ^ reversed_bits(row // rows, bits)) * rows + row % rows
    project(
        start, context_ref, w_ref, keep_ref, send_ref, buffer, arrived,
        prologue=lambda: attend(token, q_ref, kv_ref, context_ref),
    )


def next_kernel(start, context_ref, w_ref, keep_ref, send_ref, buffer, arrived):
    project(start, context_ref, w_ref, keep_ref, send_ref, buffer, arrived)


def projection_call(kernel, inputs, in_specs, total_rows, depth, width, with_context):
    half = total_rows // 2
    tile = 512
    out_shape = [
        jax.ShapeDtypeStruct((half, width), jnp.float32),
        jax.ShapeDtypeStruct((half, width), jnp.bfloat16),
    ]
    if with_context:
        out_shape = [jax.ShapeDtypeStruct((total_rows, depth), jnp.bfloat16)] + out_shape
    return pl.pallas_call(
        kernel,
        in_specs=in_specs,
        out_specs=[pl.BlockSpec(memory_space=pltpu.VMEM)] * len(out_shape),
        out_shape=out_shape,
        scratch_shapes=[
            pltpu.VMEM((width // tile, depth, tile), jnp.bfloat16),
            pltpu.SemaphoreType.DMA((width // tile,)),
        ],
        compiler_params=pltpu.CompilerParams(vmem_limit_bytes=28 << 20),
        cost_estimate=pl.CostEstimate(
            flops=2 * total_rows * depth * width,
            bytes_accessed=2 * depth * width,
            transcendentals=0,
        ),
    )(*inputs)


def finish_kernel(codes_ref, exponents_ref, *refs):
    *pieces, out_ref = refs
    rows, width = out_ref.shape
    blocks = width // HBLK
    i = lax.broadcasted_iota(jnp.int32, (HBLK, HBLK), 0)
    common = i & lax.broadcasted_iota(jnp.int32, (HBLK, HBLK), 1)
    parity = jnp.zeros((HBLK, HBLK), jnp.int32)
    for bit in range(HBLK.bit_length() - 1):
        parity = parity ^ (common >> bit)
    table = (1 - 2 * (parity & 1)).astype(jnp.bfloat16)
    scale = jnp.exp2(exponents_ref[...].astype(jnp.float32))
    at = 0
    for keep_ref, got_ref in zip(pieces[::2], pieces[1::2]):
        summed = keep_ref[...] + got_ref[...].astype(jnp.float32)
        count = summed.shape[1] // HBLK
        stacked = jnp.concatenate([summed[:, b * HBLK:(b + 1) * HBLK] for b in range(count)], axis=0)
        rotated = jnp.zeros_like(stacked)
        rest = stacked
        for _ in range(3):
            piece = rest.astype(jnp.bfloat16)
            rotated = rotated + jnp.dot(piece, table, preferred_element_type=jnp.float32)
            rest = rest - piece.astype(jnp.float32)
        rotated = rotated * (1.0 / math.sqrt(HBLK))
        for b in range(count):
            block = at + b
            columns = slice(block * HBLK, (block + 1) * HBLK)
            residual = codes_ref[:, columns].astype(jnp.float32) * scale[:, block:block + 1]
            out_ref[:, columns] = (residual + rotated[b * rows:(b + 1) * rows]).astype(jnp.bfloat16)
        at += count


def finish(codes, exponents, pieces):
    rows, width = codes.shape
    padded = max(rows, 8)
    inputs = [codes, exponents, *pieces]
    if padded != rows:
        inputs = [jnp.pad(x, ((0, padded - rows), (0, 0))) for x in inputs]
    out = pl.pallas_call(
        finish_kernel,
        out_shape=jax.ShapeDtypeStruct((padded, width), jnp.bfloat16),
        in_specs=[pl.BlockSpec(memory_space=pltpu.VMEM)] * len(inputs),
        out_specs=pl.BlockSpec(memory_space=pltpu.VMEM),
        compiler_params=pltpu.CompilerParams(vmem_limit_bytes=16 << 20),
        cost_estimate=pl.CostEstimate(flops=6 * padded * width * HBLK, bytes_accessed=12 * padded * width, transcendentals=0),
    )(*inputs)
    return out[:rows]


def passed_across(value, axis, mask):
    return lax.ppermute(value, axis, [(source, source ^ mask) for source in range(lax.axis_size(axis))])


def body(encoded_query_rows, encoded_key_rows, head_value_rows, quant_codes, exponents, out_weight):
    total_rows, query_width = encoded_query_rows.shape
    depth, width = out_weight.shape
    devices = lax.axis_size("tensor")
    bits = devices.bit_length() - 1
    local_heads = query_width // HEAD_SIZE
    query_group = QUERY_HEADS // KEY_VALUE_HEADS
    kv_rows = encoded_key_rows.shape[0]

    wanted = [device * local_heads // query_group for device in range(devices)]
    packed = jnp.stack(
        [
            jnp.concatenate(
                [x[:, head * HEAD_SIZE:(head + 1) * HEAD_SIZE] for x in (encoded_key_rows, head_value_rows)], axis=1
            )
            for head in wanted
        ]
    )
    kv = lax.all_to_all(packed, "tensor", 0, 0).reshape(devices * kv_rows, 2 * HEAD_SIZE)

    place = lax.axis_index("tensor").astype(jnp.int32).reshape(1)
    vmem = pl.BlockSpec(memory_space=pltpu.VMEM)
    anywhere = pl.BlockSpec(memory_space=pl.ANY)
    unit = width // sum(PARTS)
    start = 0
    context = None
    halves = []
    for part in PARTS:
        if context is None:
            context, keep, send = projection_call(
                functools.partial(first_kernel, start, bits),
                (place, encoded_query_rows, kv, out_weight),
                [pl.BlockSpec(memory_space=pltpu.SMEM), vmem, vmem, anywhere],
                total_rows, depth, part * unit, True,
            )
        else:
            keep, send = projection_call(
                functools.partial(next_kernel, start),
                (context, out_weight), [vmem, anywhere],
                total_rows, depth, part * unit, False,
            )
        halves.append((keep, send))
        start += part * unit

    pieces = []
    for keep, send in halves:
        for bit in range(bits):
            got = passed_across(send, "tensor", 1 << bit)
            if bit == bits - 1:
                pieces += [keep, got]
            else:
                summed = keep + got.astype(jnp.float32)
                half = summed.shape[0] // 2
                keep, send = summed[:half], summed[half:].astype(jnp.bfloat16)
    return finish(quant_codes, exponents, pieces)


def solution(mesh):
    return jax.shard_map(
        body,
        mesh=mesh,
        in_specs=(
            P("groups", "tensor"),
            P(("groups", "tensor"), None),
            P(("groups", "tensor"), None),
            P(("groups", "tensor"), None),
            P(("groups", "tensor"), None),
            P("tensor", None),
        ),
        out_specs=P(("groups", "tensor"), None),
        check_vma=False,
    )
```

```python
import functools
import math

import jax
import jax.numpy as jnp
from jax import lax
from jax.experimental import pallas as pl
from jax.experimental.pallas import tpu as pltpu
from jax.sharding import PartitionSpec as P

QUERY_HEADS = 128
KEY_VALUE_HEADS = 8
HEAD_SIZE = 128
HBLK = 128
masked_score = -1e30

LIMIT = 20 << 20
PARTS = ((4, 'yz', 8), (5, 'yz', 3), (5, 'yz', 3), (2, 'yz', 4))
AHEAD = (3, 3, 2)
TILE = 512
SPLIT = {}
EVENTS = ((0, 0), (1, -1), (0, 1), (1, 0), (2, -1), (0, 2), (1, 1), (2, 0), (3, -1), (1, 2), (2, 1), (0, 3), (3, 0), (2, 2), (3, 1), (1, 3), (0, 4), (3, 2), (2, 3), (1, 4), (3, 3), (2, 4), (3, 4))


def events(bits):
    if bits == 4:
        return EVENTS
    steps = range(-1, bits + 1)
    return [(part, step) for step in steps for part, (_, _, ahead) in enumerate(PARTS) if step >= 0 or (part and ahead)]


def halving_order(kind, bits):
    if kind == "yz":
        return list(range(bits))
    if kind == "zyz":
        return [0, 2, 1, *range(3, bits)]
    return [0, *range(2, bits), 1]


def reversed_bits(index, bits):
    result = 0
    for bit in range(bits):
        result = result + ((index >> bit) & 1) * (1 << (bits - 1 - bit))
    return result


def fetches(start, w_ref, buffer_ref, arrived):
    tiles, _, tile = buffer_ref.shape
    return [
        pltpu.make_async_copy(w_ref.at[:, pl.ds(start + index * tile, tile)], buffer_ref.at[index], arrived.at[index])
        for index in range(tiles)
    ]


def prepare_kernel(bits, place_ref, q_ref, queries_ref, held, arrived):
    copy = pltpu.make_async_copy(q_ref, held, arrived)
    copy.start()
    total_rows = q_ref.shape[0]
    column = lax.broadcasted_iota(jnp.int32, (total_rows, total_rows), 1)
    order = jnp.where(column == token_of_row(place_ref, total_rows, bits), 1.0, 0.0).astype(jnp.bfloat16)
    copy.wait()
    queries_ref[...] = jnp.dot(order, held[...], preferred_element_type=jnp.float32).astype(jnp.bfloat16)


def token_of_row(place_ref, total_rows, bits):
    rows = total_rows >> bits
    row = lax.broadcasted_iota(jnp.int32, (total_rows, 1), 0)
    return (place_ref[0] ^ reversed_bits(row // rows, bits)) * rows + row % rows


def attend(bits, place_ref, queries_ref, kv_ref, context_ref):
    total_rows = queries_ref.shape[0]
    visible = key_tokens(place_ref, bits, (total_rows, total_rows)) <= token_of_row(place_ref, total_rows, bits)
    key = kv_ref[:, :HEAD_SIZE]
    value = kv_ref[:, HEAD_SIZE:]
    for head in range(queries_ref.shape[1] // HEAD_SIZE):
        columns = slice(head * HEAD_SIZE, (head + 1) * HEAD_SIZE)
        scores = lax.dot_general(
            queries_ref[:, columns], key, (((1,), (1,)), ((), ())), preferred_element_type=jnp.float32
        ) * (1.0 / math.sqrt(HEAD_SIZE))
        scores = jnp.where(visible, scores, masked_score)
        top = jnp.max(scores, axis=1, keepdims=True)
        weights = jnp.where(visible, jnp.exp(scores - top), 0.0)
        total = jnp.sum(weights, axis=1, keepdims=True)
        high = weights.astype(jnp.bfloat16)
        low = (weights - high.astype(jnp.float32)).astype(jnp.bfloat16)
        weighted = jnp.dot(high, value, preferred_element_type=jnp.float32)
        weighted = weighted + jnp.dot(low, value, preferred_element_type=jnp.float32)
        context_ref[:, columns] = (weighted / total).astype(jnp.bfloat16)


def fetch_kernel(start, place_ref, w_ref, buffer_ref, arrived):
    copies = fetches(start, w_ref, buffer_ref, arrived)
    for copy in copies:
        copy.start()
    for copy in copies:
        copy.wait()


def multiply(context_ref, weight, at, keep_ref, send_ref):
    half = keep_ref.shape[0]
    columns = slice(at, at + weight.shape[1])
    product = jnp.dot(context_ref[...], weight, preferred_element_type=jnp.float32)
    keep_ref[:, columns] = product[:half]
    send_ref[:, columns] = product[half:].astype(jnp.bfloat16)


def part_kernel(bits, start, with_attention, *refs):
    if with_attention:
        place_ref, queries_ref, kv_ref, w_ref, *refs = refs
        *ahead_refs, context_ref, keep_ref, send_ref, buffer, arrived = refs
    else:
        context_ref, w_ref, *refs = refs
        *ahead_refs, keep_ref, send_ref, buffer, arrived = refs
    tiles = [(ref, index) for ref in ahead_refs for index in range(ref.shape[0])]
    missing = keep_ref.shape[1] // TILE - len(tiles)
    copies = fetches(start + len(tiles) * TILE, w_ref, buffer, arrived) if missing else []
    for copy in copies:
        copy.start()
    if with_attention:
        attend(bits, place_ref, queries_ref, kv_ref, context_ref)
    for index, (ref, tile) in enumerate(tiles):
        multiply(context_ref, ref[tile], index * TILE, keep_ref, send_ref)
    for index, copy in enumerate(copies):
        copy.wait()
        multiply(context_ref, buffer[index], (len(tiles) + index) * TILE, keep_ref, send_ref)


VMEM = pl.BlockSpec(memory_space=pltpu.VMEM)
SMEM = pl.BlockSpec(memory_space=pltpu.SMEM)
ANYWHERE = pl.BlockSpec(memory_space=pl.ANY)


def prepare(place, queries, bits):
    return pl.pallas_call(
        functools.partial(prepare_kernel, bits),
        in_specs=[SMEM, ANYWHERE],
        out_specs=VMEM,
        out_shape=jax.ShapeDtypeStruct(queries.shape, queries.dtype),
        scratch_shapes=[pltpu.VMEM(queries.shape, queries.dtype), pltpu.SemaphoreType.DMA],
        compiler_params=pltpu.CompilerParams(vmem_limit_bytes=LIMIT),
        cost_estimate=pl.CostEstimate(flops=0, bytes_accessed=4 * queries.size, transcendentals=0),
    )(place, queries)


def fetch(place, weight, start, tiles):
    return pl.pallas_call(
        functools.partial(fetch_kernel, start),
        in_specs=[SMEM, ANYWHERE],
        out_specs=VMEM,
        out_shape=jax.ShapeDtypeStruct((tiles, weight.shape[0], TILE), weight.dtype),
        scratch_shapes=[pltpu.SemaphoreType.DMA((tiles,))],
        compiler_params=pltpu.CompilerParams(vmem_limit_bytes=LIMIT),
    )(place, weight)


def project_part(bits, start, columns, context, first_inputs, weight, ahead):
    with_attention = context is None
    depth = weight.shape[0]
    total_rows = (first_inputs[1] if with_attention else context).shape[0]
    missing = max(columns // TILE - sum(array.shape[0] for array in ahead), 1)
    out_shape = [
        jax.ShapeDtypeStruct((total_rows // 2, columns), jnp.float32),
        jax.ShapeDtypeStruct((total_rows // 2, columns), jnp.bfloat16),
    ]
    inputs, in_specs = [context, weight], [VMEM, ANYWHERE]
    if with_attention:
        out_shape = [jax.ShapeDtypeStruct((total_rows, depth), jnp.bfloat16)] + out_shape
        inputs, in_specs = [*first_inputs, weight], [SMEM, VMEM, VMEM, ANYWHERE]
    return pl.pallas_call(
        functools.partial(part_kernel, bits, start, with_attention),
        in_specs=in_specs + [VMEM] * len(ahead),
        out_specs=[VMEM] * len(out_shape),
        out_shape=out_shape,
        scratch_shapes=[pltpu.VMEM((missing, depth, TILE), jnp.bfloat16), pltpu.SemaphoreType.DMA((missing,))],
        compiler_params=pltpu.CompilerParams(vmem_limit_bytes=LIMIT),
    )(*inputs, *ahead)


def finish_kernel(bounds, codes_ref, exponents_ref, *refs):
    *pieces, out_ref = refs
    rows = out_ref.shape[0]
    i = lax.broadcasted_iota(jnp.int32, (HBLK, HBLK), 0)
    common = i & lax.broadcasted_iota(jnp.int32, (HBLK, HBLK), 1)
    parity = jnp.zeros((HBLK, HBLK), jnp.int32)
    for bit in range(HBLK.bit_length() - 1):
        parity = parity ^ (common >> bit)
    table = (1 - 2 * (parity & 1)).astype(jnp.bfloat16)
    scale = jnp.exp2(exponents_ref[...].astype(jnp.float32))
    for start, keep_ref, got_ref in zip(bounds, pieces[::2], pieces[1::2]):
        summed = keep_ref[...] + got_ref[...].astype(jnp.float32)
        blocks = summed.shape[1] // HBLK
        rest = jnp.concatenate([summed[:, b * HBLK:(b + 1) * HBLK] for b in range(blocks)], axis=0)
        rotated = jnp.zeros_like(rest)
        for _ in range(3):
            piece = rest.astype(jnp.bfloat16)
            rotated = rotated + jnp.dot(piece, table, preferred_element_type=jnp.float32)
            rest = rest - piece.astype(jnp.float32)
        rotated = rotated * (1.0 / math.sqrt(HBLK))
        for b in range(blocks):
            block = start // HBLK + b
            columns = slice(block * HBLK, (block + 1) * HBLK)
            residual = codes_ref[:, columns].astype(jnp.float32) * scale[:, block:block + 1]
            out_ref[:, columns] = (residual + rotated[b * rows:(b + 1) * rows]).astype(jnp.bfloat16)


def finish(codes, exponents, pieces, bounds):
    rows, width = codes.shape
    spare = max(8 - rows, 0)
    inputs = [jnp.pad(x, ((0, spare), (0, 0))) for x in (codes, exponents, *pieces)]
    out = pl.pallas_call(
        functools.partial(finish_kernel, bounds),
        in_specs=[VMEM] * len(inputs),
        out_specs=VMEM,
        out_shape=jax.ShapeDtypeStruct((rows + spare, width), jnp.bfloat16),
        compiler_params=pltpu.CompilerParams(vmem_limit_bytes=LIMIT),
    )(*inputs)
    return out[:rows]


def passed_across(value, axis, mask):
    return lax.ppermute(value, axis, [(source, source ^ mask) for source in range(lax.axis_size(axis))])


def pack_kernel(local_heads, place_ref, key_ref, value_ref, packed_ref, held, arrived):
    copies = [
        pltpu.make_async_copy(ref, held.at[index], arrived.at[index]) for index, ref in enumerate((key_ref, value_ref))
    ]
    for copy in copies:
        copy.start()
    for copy in copies:
        copy.wait()
    query_group = QUERY_HEADS // KEY_VALUE_HEADS
    chip = place_ref[0] // 2
    for away in range(packed_ref.shape[0]):
        head = (chip ^ away) * 2 * local_heads // query_group
        columns = pl.ds(pl.multiple_of(head * HEAD_SIZE, HEAD_SIZE), HEAD_SIZE)
        for index in range(2):
            packed_ref[away, :, index * HEAD_SIZE:(index + 1) * HEAD_SIZE] = held[index, :, columns]


def shared_out(place, key_rows, value_rows, weight, bits, local_heads):
    rows = key_rows.shape[0]
    chips = 1 << (bits - 1)
    packed = pl.pallas_call(
        functools.partial(pack_kernel, local_heads),
        out_shape=jax.ShapeDtypeStruct((chips, rows, 2 * HEAD_SIZE), key_rows.dtype),
        in_specs=[SMEM, ANYWHERE, ANYWHERE],
        out_specs=VMEM,
        scratch_shapes=[pltpu.VMEM((2, *key_rows.shape), key_rows.dtype), pltpu.SemaphoreType.DMA((2,))],
        compiler_params=pltpu.CompilerParams(vmem_limit_bytes=LIMIT),
    )(place, *(pltpu.with_memory_space_constraint(x, pltpu.HBM) for x in (key_rows, value_rows)))
    held = packed[:, None]
    ahead = []
    fetched = 0
    for bit in range(bits - 1):
        halves = held.reshape(-1, 2, *held.shape[1:])
        keep, send = halves[:, 0], halves[:, 1]
        got = passed_across(send, "tensor", 2 << bit)
        if bit < len(AHEAD):
            now, _ = lax.optimization_barrier((place, send))
            ahead.append(fetch(now, weight, fetched * TILE, AHEAD[bit]))
            fetched += AHEAD[bit]
            keep, got, ahead[-1] = lax.optimization_barrier((keep, got, ahead[-1]))
        held = jnp.concatenate([keep, got], axis=1)
    held = held[0]
    got = passed_across(held, "tensor", 1)
    return jnp.concatenate([held, got], axis=0).reshape(2 * chips * rows, 2 * HEAD_SIZE), ahead


def key_tokens(place_ref, bits, shape):
    index = lax.broadcasted_iota(jnp.int32, shape, 1)
    rows = shape[1] >> bits
    block = index // rows
    chips = 1 << (bits - 1)
    away = block // chips + 2 * (block % chips)
    return (place_ref[0] ^ away) * rows + index % rows


def body(encoded_query_rows, encoded_key_rows, head_value_rows, quant_codes, exponents, out_weight):
    total_rows, query_width = encoded_query_rows.shape
    depth, width = out_weight.shape
    devices = lax.axis_size("tensor")
    bits = devices.bit_length() - 1
    local_heads = query_width // HEAD_SIZE
    rows = total_rows // devices

    place = lax.axis_index("tensor").astype(jnp.int32).reshape(1)
    weight = pltpu.with_memory_space_constraint(out_weight, pltpu.HBM)
    queries = prepare(place, encoded_query_rows, bits)
    kv, ahead = shared_out(place, encoded_key_rows, head_value_rows, weight, bits, local_heads)
    unit = width // sum(columns for columns, *_ in PARTS)
    starts = [unit * sum(columns for columns, *_ in PARTS[:part]) for part in range(len(PARTS))]

    context = token = None
    state = {}
    fetched = {0: ahead}
    for part, step in events(bits):
        columns, order, tiles = PARTS[part]
        columns *= unit
        order = halving_order(order, bits)
        if step == -2:
            left, keep, got = state[part]
            *early, token = lax.optimization_barrier((*got[:-1], token))
            state[part] = left, keep, [*early, got[-1]]
            continue
        if step == -1:
            now = place if token is None else lax.optimization_barrier((place, token))[0]
            token = fetch(now, weight, starts[part], tiles)
            fetched[part] = [token]
            continue
        if step == 0:
            if context is None:
                context, keep, send = project_part(bits, starts[part], columns, None, (place, queries, kv), weight, ahead)
            else:
                held, token = lax.optimization_barrier((context, token))
                keep, send = project_part(bits, starts[part], columns, held, None, weight, fetched.get(part, []))
            left = list(range(1, bits))
        else:
            left, keep, got = state[part]
            keep, token, *got = lax.optimization_barrier((keep, token, *got))
            if step == bits:
                state[part] = left, keep, got
                token = got[0]
                continue
            bounds = [sum(piece.shape[1] for piece in got[:i]) for i in range(len(got) + 1)]
            summed = jnp.concatenate(
                [
                    keep[:, begin:end] + piece.astype(jnp.float32)
                    for begin, end, piece in zip(bounds, bounds[1:], got)
                ],
                axis=1,
            ).reshape((2,) * len(left) + (rows, columns))
            axis = left.index(order[step])
            keep, send = (
                lax.index_in_dim(summed, side, axis, keepdims=False).reshape(-1, columns) for side in (0, 1)
            )
            send = send.astype(jnp.bfloat16)
            left = left[:axis] + left[axis + 1:]
        token = send
        cuts = [columns]
        if bits == 4 and step < 2:
            cuts = SPLIT.get((part, step), cuts)
        ends = [0, *(cut * TILE for cut in cuts if cut * TILE < columns), columns]
        pieces = [send[:, begin:end] for begin, end in zip(ends, ends[1:])]
        state[part] = left, keep, [passed_across(piece, "tensor", 1 << order[step]) for piece in pieces]
    pieces = [array for part in range(len(PARTS)) for array in (state[part][1], state[part][2][0])]
    return finish(quant_codes, exponents, pieces, starts)


def solution(mesh):
    return jax.shard_map(
        body,
        mesh=mesh,
        in_specs=(
            P("groups", "tensor"),
            P(("groups", "tensor"), None),
            P(("groups", "tensor"), None),
            P(("groups", "tensor"), None),
            P(("groups", "tensor"), None),
            P("tensor", None),
        ),
        out_specs=P(("groups", "tensor"), None),
        check_vma=False,
    )
```

```python
import functools
import math

import jax
import jax.numpy as jnp
from jax import lax
from jax.experimental import pallas as pl
from jax.experimental.pallas import tpu as pltpu
from jax.sharding import PartitionSpec as P

QUERY_HEADS = 128
KEY_VALUE_HEADS = 8
HEAD_SIZE = 128
HBLK = 128
masked_score = -1e30

LIMIT = 12 << 20
PARTS = ((4, 'yz', 8), (5, 'yz', 3), (4, 'zyz', 0), (3, 'yz', 3))
AHEAD = (4, 4)
TILE = 512
SPLIT = {}
EVENTS = ((0, 0), (1, -1), (0, 1), (1, 0), (2, 0), (0, 2), (1, 1), (2, 1), (3, -1), (3, 0), (1, 2), (3, 1), (2, 2), (0, 3), (1, 3), (3, 2), (2, 3), (0, 4), (1, 4), (3, 3), (2, 4), (3, 4))


def events(bits):
    if bits == 4:
        return EVENTS
    steps = range(-1, bits + 1)
    return [(part, step) for step in steps for part, (_, _, ahead) in enumerate(PARTS) if step >= 0 or (part and ahead)]


def halving_order(kind, bits):
    if kind == "yz":
        return list(range(bits))
    if kind == "zyz":
        return [0, 2, 1, *range(3, bits)]
    return [0, *range(2, bits), 1]


def reversed_bits(index, bits):
    result = 0
    for bit in range(bits):
        result = result + ((index >> bit) & 1) * (1 << (bits - 1 - bit))
    return result


def fetches(start, w_ref, buffer_ref, arrived):
    tiles, _, tile = buffer_ref.shape
    return [
        pltpu.make_async_copy(w_ref.at[:, pl.ds(start + index * tile, tile)], buffer_ref.at[index], arrived.at[index])
        for index in range(tiles)
    ]


def prepare_kernel(bits, place_ref, q_ref, queries_ref, held, arrived):
    copy = pltpu.make_async_copy(q_ref, held, arrived)
    copy.start()
    total_rows = q_ref.shape[0]
    column = lax.broadcasted_iota(jnp.int32, (total_rows, total_rows), 1)
    order = jnp.where(column == token_of_row(place_ref, total_rows, bits), 1.0, 0.0).astype(jnp.bfloat16)
    copy.wait()
    queries_ref[...] = jnp.dot(order, held[...], preferred_element_type=jnp.float32).astype(jnp.bfloat16)


def token_of_row(place_ref, total_rows, bits):
    rows = total_rows >> bits
    row = lax.broadcasted_iota(jnp.int32, (total_rows, 1), 0)
    return (place_ref[0] ^ reversed_bits(row // rows, bits)) * rows + row % rows


def attend(bits, place_ref, queries_ref, kv_ref, context_ref):
    total_rows = queries_ref.shape[0]
    visible = key_tokens(place_ref, bits, (total_rows, total_rows)) <= token_of_row(place_ref, total_rows, bits)
    key = kv_ref[:, :HEAD_SIZE]
    value = kv_ref[:, HEAD_SIZE:]
    for head in range(queries_ref.shape[1] // HEAD_SIZE):
        columns = slice(head * HEAD_SIZE, (head + 1) * HEAD_SIZE)
        scores = lax.dot_general(
            queries_ref[:, columns], key, (((1,), (1,)), ((), ())), preferred_element_type=jnp.float32
        ) * (1.0 / math.sqrt(HEAD_SIZE))
        scores = jnp.where(visible, scores, masked_score)
        top = jnp.max(scores, axis=1, keepdims=True)
        weights = jnp.where(visible, jnp.exp(scores - top), 0.0)
        total = jnp.sum(weights, axis=1, keepdims=True)
        high = weights.astype(jnp.bfloat16)
        low = (weights - high.astype(jnp.float32)).astype(jnp.bfloat16)
        weighted = jnp.dot(high, value, preferred_element_type=jnp.float32)
        weighted = weighted + jnp.dot(low, value, preferred_element_type=jnp.float32)
        context_ref[:, columns] = (weighted / total).astype(jnp.bfloat16)


def fetch_kernel(start, place_ref, w_ref, buffer_ref, arrived):
    copies = fetches(start, w_ref, buffer_ref, arrived)
    for copy in copies:
        copy.start()
    for copy in copies:
        copy.wait()


def multiply(context_ref, weight, at, keep_ref, send_ref):
    half = keep_ref.shape[0]
    columns = slice(at, at + weight.shape[1])
    product = jnp.dot(context_ref[...], weight, preferred_element_type=jnp.float32)
    keep_ref[:, columns] = product[:half]
    send_ref[:, columns] = product[half:].astype(jnp.bfloat16)


def part_kernel(bits, start, with_attention, *refs):
    if with_attention:
        place_ref, queries_ref, kv_ref, w_ref, *refs = refs
        *ahead_refs, context_ref, keep_ref, send_ref, buffer, arrived = refs
    else:
        context_ref, w_ref, *refs = refs
        *ahead_refs, keep_ref, send_ref, buffer, arrived = refs
    tiles = [(ref, index) for ref in ahead_refs for index in range(ref.shape[0])]
    missing = keep_ref.shape[1] // TILE - len(tiles)
    copies = fetches(start + len(tiles) * TILE, w_ref, buffer, arrived) if missing else []
    for copy in copies:
        copy.start()
    if with_attention:
        attend(bits, place_ref, queries_ref, kv_ref, context_ref)
    for index, (ref, tile) in enumerate(tiles):
        multiply(context_ref, ref[tile], index * TILE, keep_ref, send_ref)
    for index, copy in enumerate(copies):
        copy.wait()
        multiply(context_ref, buffer[index], (len(tiles) + index) * TILE, keep_ref, send_ref)


VMEM = pl.BlockSpec(memory_space=pltpu.VMEM)
SMEM = pl.BlockSpec(memory_space=pltpu.SMEM)
ANYWHERE = pl.BlockSpec(memory_space=pl.ANY)


def prepare(place, queries, bits):
    return pl.pallas_call(
        functools.partial(prepare_kernel, bits),
        in_specs=[SMEM, ANYWHERE],
        out_specs=VMEM,
        out_shape=jax.ShapeDtypeStruct(queries.shape, queries.dtype),
        scratch_shapes=[pltpu.VMEM(queries.shape, queries.dtype), pltpu.SemaphoreType.DMA],
        compiler_params=pltpu.CompilerParams(vmem_limit_bytes=LIMIT),
        cost_estimate=pl.CostEstimate(flops=0, bytes_accessed=4 * queries.size, transcendentals=0),
    )(place, queries)


def fetch(place, weight, start, tiles):
    return pl.pallas_call(
        functools.partial(fetch_kernel, start),
        in_specs=[SMEM, ANYWHERE],
        out_specs=VMEM,
        out_shape=jax.ShapeDtypeStruct((tiles, weight.shape[0], TILE), weight.dtype),
        scratch_shapes=[pltpu.SemaphoreType.DMA((tiles,))],
        compiler_params=pltpu.CompilerParams(vmem_limit_bytes=LIMIT),
    )(place, weight)


def project_part(bits, start, columns, context, first_inputs, weight, ahead):
    with_attention = context is None
    depth = weight.shape[0]
    total_rows = (first_inputs[1] if with_attention else context).shape[0]
    missing = max(columns // TILE - sum(array.shape[0] for array in ahead), 1)
    out_shape = [
        jax.ShapeDtypeStruct((total_rows // 2, columns), jnp.float32),
        jax.ShapeDtypeStruct((total_rows // 2, columns), jnp.bfloat16),
    ]
    inputs, in_specs = [context, weight], [VMEM, ANYWHERE]
    if with_attention:
        out_shape = [jax.ShapeDtypeStruct((total_rows, depth), jnp.bfloat16)] + out_shape
        inputs, in_specs = [*first_inputs, weight], [SMEM, VMEM, VMEM, ANYWHERE]
    return pl.pallas_call(
        functools.partial(part_kernel, bits, start, with_attention),
        in_specs=in_specs + [VMEM] * len(ahead),
        out_specs=[VMEM] * len(out_shape),
        out_shape=out_shape,
        scratch_shapes=[pltpu.VMEM((missing, depth, TILE), jnp.bfloat16), pltpu.SemaphoreType.DMA((missing,))],
        compiler_params=pltpu.CompilerParams(vmem_limit_bytes=LIMIT),
    )(*inputs, *ahead)


def finish_kernel(bounds, codes_ref, exponents_ref, *refs):
    pieces = refs[:2 * len(bounds)]
    out_ref, *done_refs, stored = refs[len(refs) - len(bounds) - 2:]
    i = lax.broadcasted_iota(jnp.int32, (HBLK, HBLK), 0)
    common = i & lax.broadcasted_iota(jnp.int32, (HBLK, HBLK), 1)
    parity = jnp.zeros((HBLK, HBLK), jnp.int32)
    for bit in range(HBLK.bit_length() - 1):
        parity = parity ^ (common >> bit)
    table = (1 - 2 * (parity & 1)).astype(jnp.bfloat16)
    scale = jnp.exp2(exponents_ref[...].astype(jnp.float32))
    stores = []
    for index, (start, keep_ref, got_ref, done_ref) in enumerate(zip(bounds, pieces[::2], pieces[1::2], done_refs)):
        rows, width = done_ref.shape
        summed = keep_ref[...] + got_ref[...].astype(jnp.float32)
        blocks = width // HBLK
        rest = jnp.concatenate([summed[:, b * HBLK:(b + 1) * HBLK] for b in range(blocks)], axis=0)
        rotated = jnp.zeros_like(rest)
        for _ in range(3):
            piece = rest.astype(jnp.bfloat16)
            rotated = rotated + jnp.dot(piece, table, preferred_element_type=jnp.float32)
            rest = rest - piece.astype(jnp.float32)
        rotated = rotated * (1.0 / math.sqrt(HBLK))
        for b in range(blocks):
            block = start // HBLK + b
            codes = codes_ref[:, block * HBLK:(block + 1) * HBLK].astype(jnp.float32)
            done_ref[:, b * HBLK:(b + 1) * HBLK] = (
                codes * scale[:, block:block + 1] + rotated[b * rows:(b + 1) * rows]
            ).astype(jnp.bfloat16)
        store = pltpu.make_async_copy(done_ref, out_ref.at[:, pl.ds(start, width)], stored.at[index])
        store.start()
        stores.append(store)
    for store in stores:
        store.wait()


def finish(codes, exponents, pieces, bounds, out):
    inputs, in_specs, aliases = [codes, exponents, *pieces], [VMEM] * (2 + len(pieces)), {}
    if out is not None:
        aliases = {len(inputs): 0}
        inputs, in_specs = [*inputs, out], [*in_specs, ANYWHERE]
    return pl.pallas_call(
        functools.partial(finish_kernel, bounds),
        in_specs=in_specs,
        out_specs=ANYWHERE,
        out_shape=jax.ShapeDtypeStruct(codes.shape, jnp.bfloat16),
        input_output_aliases=aliases,
        scratch_shapes=[pltpu.VMEM(keep.shape, jnp.bfloat16) for keep in pieces[::2]]
        + [pltpu.SemaphoreType.DMA((len(bounds),))],
        compiler_params=pltpu.CompilerParams(vmem_limit_bytes=LIMIT),
    )(*inputs)


def passed_across(value, axis, mask):
    return lax.ppermute(value, axis, [(source, source ^ mask) for source in range(lax.axis_size(axis))])


def pack_kernel(local_heads, place_ref, key_ref, value_ref, packed_ref, held, arrived):
    copies = [
        pltpu.make_async_copy(ref, held.at[index], arrived.at[index]) for index, ref in enumerate((key_ref, value_ref))
    ]
    for copy in copies:
        copy.start()
    for copy in copies:
        copy.wait()
    query_group = QUERY_HEADS // KEY_VALUE_HEADS
    chip = place_ref[0] // 2
    for away in range(packed_ref.shape[0]):
        head = (chip ^ away) * 2 * local_heads // query_group
        columns = pl.ds(pl.multiple_of(head * HEAD_SIZE, HEAD_SIZE), HEAD_SIZE)
        for index in range(2):
            packed_ref[away, :, index * HEAD_SIZE:(index + 1) * HEAD_SIZE] = held[index, :, columns]


def shared_out(place, key_rows, value_rows, weight, bits, local_heads):
    rows = key_rows.shape[0]
    chips = 1 << (bits - 1)
    packed = pl.pallas_call(
        functools.partial(pack_kernel, local_heads),
        out_shape=jax.ShapeDtypeStruct((chips, rows, 2 * HEAD_SIZE), key_rows.dtype),
        in_specs=[SMEM, ANYWHERE, ANYWHERE],
        out_specs=VMEM,
        scratch_shapes=[pltpu.VMEM((2, *key_rows.shape), key_rows.dtype), pltpu.SemaphoreType.DMA((2,))],
        compiler_params=pltpu.CompilerParams(vmem_limit_bytes=LIMIT),
    )(place, *(pltpu.with_memory_space_constraint(x, pltpu.HBM) for x in (key_rows, value_rows)))
    held = packed[:, None]
    ahead = []
    fetched = 0
    for bit in range(bits - 1):
        halves = held.reshape(-1, 2, *held.shape[1:])
        keep, send = halves[:, 0], halves[:, 1]
        got = passed_across(send, "tensor", 2 << bit)
        if bit < len(AHEAD):
            now, _ = lax.optimization_barrier((place, send))
            ahead.append(fetch(now, weight, fetched * TILE, AHEAD[bit]))
            fetched += AHEAD[bit]
            keep, got, ahead[-1] = lax.optimization_barrier((keep, got, ahead[-1]))
        held = jnp.concatenate([keep, got], axis=1)
    held = held[0]
    got = passed_across(held, "tensor", 1)
    return jnp.concatenate([held, got], axis=0).reshape(2 * chips * rows, 2 * HEAD_SIZE), ahead


def key_tokens(place_ref, bits, shape):
    index = lax.broadcasted_iota(jnp.int32, shape, 1)
    rows = shape[1] >> bits
    block = index // rows
    chips = 1 << (bits - 1)
    away = block // chips + 2 * (block % chips)
    return (place_ref[0] ^ away) * rows + index % rows


def body(encoded_query_rows, encoded_key_rows, head_value_rows, quant_codes, exponents, out_weight):
    total_rows, query_width = encoded_query_rows.shape
    depth, width = out_weight.shape
    devices = lax.axis_size("tensor")
    bits = devices.bit_length() - 1
    local_heads = query_width // HEAD_SIZE
    rows = total_rows // devices

    place = lax.axis_index("tensor").astype(jnp.int32).reshape(1)
    weight = pltpu.with_memory_space_constraint(out_weight, pltpu.HBM)
    queries = prepare(place, encoded_query_rows, bits)
    kv, ahead = shared_out(place, encoded_key_rows, head_value_rows, weight, bits, local_heads)
    unit = width // sum(columns for columns, *_ in PARTS)
    starts = [unit * sum(columns for columns, *_ in PARTS[:part]) for part in range(len(PARTS))]

    context = token = None
    state = {}
    fetched = {0: ahead}

    def summed_halves(part, step):
        nonlocal token
        left, keep, got = state.pop(part)
        keep, got, token = lax.optimization_barrier((keep, got, token))
        got = got[0] if len(got) == 1 else jnp.concatenate(got, axis=1)
        if step == bits:
            return left, keep, got
        columns = keep.shape[1]
        summed = (keep + got.astype(jnp.float32)).reshape((2,) * len(left) + (rows, columns))
        axis = left.index(halving_order(PARTS[part][1], bits)[step])
        keep, send = (lax.index_in_dim(summed, side, axis, keepdims=False).reshape(-1, columns) for side in (0, 1))
        return left[:axis] + left[axis + 1:], keep, send.astype(jnp.bfloat16)

    for part, step, *joined in events(bits):
        columns, order, tiles = PARTS[part]
        columns *= unit
        if step == -2:
            left, keep, got = state[part]
            early, token = lax.optimization_barrier((got[0], token))
            state[part] = left, keep, (early, *got[1:])
            continue
        if step == -1:
            now = place if token is None else lax.optimization_barrier((place, token))[0]
            token = fetch(now, weight, starts[part], tiles)
            fetched[part] = [token]
            continue
        if step == 0:
            if context is None:
                context, keep, send = project_part(bits, starts[part], columns, None, (place, queries, kv), weight, ahead)
            else:
                held, token = lax.optimization_barrier((context, token))
                keep, send = project_part(bits, starts[part], columns, held, None, weight, fetched.get(part, []))
            left = list(range(1, bits))
        else:
            left, keep, send = summed_halves(part, step)
            for other in joined:
                _, keep_too, send_too = summed_halves(other, step)
                keep = jnp.concatenate([keep, keep_too], axis=1)
                send = jnp.concatenate([send, send_too], axis=1)
        if step == bits:
            state[part], token = (left, keep, send), send
            continue
        cut = SPLIT.get(part, 0) * TILE if step == 1 else 0
        token = (send[:, :cut], send[:, cut:]) if cut else (send,)
        mask = 1 << halving_order(order, bits)[step]
        state[part] = left, keep, tuple(passed_across(piece, "tensor", mask) for piece in token)
    spare = max(8 - rows, 0)
    codes, scales = (jnp.pad(x, ((0, spare), (0, 0))) for x in (quant_codes, exponents))
    *early, last = state
    out = None
    for group in (early, [last]):
        if group:
            pieces = [jnp.pad(x, ((0, spare), (0, 0))) for part in group for x in state[part][1:]]
            out = finish(codes, scales, pieces, [starts[part] for part in group], out)
    return out[:rows]


def solution(mesh):
    return jax.shard_map(
        body,
        mesh=mesh,
        in_specs=(
            P("groups", "tensor"),
            P(("groups", "tensor"), None),
            P(("groups", "tensor"), None),
            P(("groups", "tensor"), None),
            P(("groups", "tensor"), None),
            P("tensor", None),
        ),
        out_specs=P(("groups", "tensor"), None),
        check_vma=False,
    )
```

```python
import functools
import math

import jax
import jax.numpy as jnp
from jax import lax
from jax.experimental import pallas as pl
from jax.experimental.pallas import tpu as pltpu
from jax.sharding import PartitionSpec as P

QUERY_HEADS = 128
KEY_VALUE_HEADS = 8
HEAD_SIZE = 128
HBLK = 128
masked_score = -1e30

LIMIT = 12 << 20
PARTS = ((4, 'yz', 8), (4, 'yz', 3), (5, 'zyz', 0), (3, 'yz', 3))
AHEAD = (4, 3, 1)
TILE = 512
SPLIT = {}
EVENTS = ((0, 0), (1, -1), (0, 1), (1, 0), (2, 0), (0, 2), (1, 1), (2, 1), (3, -1), (3, 0), (1, 2), (0, 3), (3, 1), (2, 2), (1, 3), (3, 2), (2, 3), (0, 4), (1, 4), (3, 3), (2, 4), (3, 4))


def events(bits):
    if bits == 4:
        return EVENTS
    steps = range(-1, bits + 1)
    return [(part, step) for step in steps for part, (_, _, ahead) in enumerate(PARTS) if step >= 0 or (part and ahead)]


def halving_order(kind, bits):
    if kind == "yz":
        return list(range(bits))
    if kind == "zyz":
        return [0, 2, 1, *range(3, bits)]
    return [0, *range(2, bits), 1]


def reversed_bits(index, bits):
    result = 0
    for bit in range(bits):
        result = result + ((index >> bit) & 1) * (1 << (bits - 1 - bit))
    return result


def fetches(start, w_ref, buffer_ref, arrived):
    tiles, _, tile = buffer_ref.shape
    return [
        pltpu.make_async_copy(w_ref.at[:, pl.ds(start + index * tile, tile)], buffer_ref.at[index], arrived.at[index])
        for index in range(tiles)
    ]


def prepare_kernel(bits, place_ref, q_ref, queries_ref, held, arrived):
    copy = pltpu.make_async_copy(q_ref, held, arrived)
    copy.start()
    total_rows = q_ref.shape[0]
    column = lax.broadcasted_iota(jnp.int32, (total_rows, total_rows), 1)
    order = jnp.where(column == token_of_row(place_ref, total_rows, bits), 1.0, 0.0).astype(jnp.bfloat16)
    copy.wait()
    queries_ref[...] = jnp.dot(order, held[...], preferred_element_type=jnp.float32).astype(jnp.bfloat16)


def token_of_row(place_ref, total_rows, bits):
    rows = total_rows >> bits
    row = lax.broadcasted_iota(jnp.int32, (total_rows, 1), 0)
    return (place_ref[0] ^ reversed_bits(row // rows, bits)) * rows + row % rows


def attend(bits, place_ref, queries_ref, kv_ref, context_ref):
    total_rows = queries_ref.shape[0]
    visible = key_tokens(place_ref, bits, (total_rows, total_rows)) <= token_of_row(place_ref, total_rows, bits)
    key = kv_ref[:, :HEAD_SIZE]
    value = kv_ref[:, HEAD_SIZE:]
    for head in range(queries_ref.shape[1] // HEAD_SIZE):
        columns = slice(head * HEAD_SIZE, (head + 1) * HEAD_SIZE)
        scores = lax.dot_general(
            queries_ref[:, columns], key, (((1,), (1,)), ((), ())), preferred_element_type=jnp.float32
        ) * (1.0 / math.sqrt(HEAD_SIZE))
        scores = jnp.where(visible, scores, masked_score)
        top = jnp.max(scores, axis=1, keepdims=True)
        weights = jnp.where(visible, jnp.exp(scores - top), 0.0)
        total = jnp.sum(weights, axis=1, keepdims=True)
        high = weights.astype(jnp.bfloat16)
        low = (weights - high.astype(jnp.float32)).astype(jnp.bfloat16)
        weighted = jnp.dot(high, value, preferred_element_type=jnp.float32)
        weighted = weighted + jnp.dot(low, value, preferred_element_type=jnp.float32)
        context_ref[:, columns] = (weighted / total).astype(jnp.bfloat16)


def fetch_kernel(start, place_ref, w_ref, buffer_ref, arrived):
    copies = fetches(start, w_ref, buffer_ref, arrived)
    for copy in copies:
        copy.start()
    for copy in copies:
        copy.wait()


def multiply(context_ref, weight, at, keep_ref, send_ref):
    half = keep_ref.shape[0]
    columns = slice(at, at + weight.shape[1])
    product = jnp.dot(context_ref[...], weight, preferred_element_type=jnp.float32)
    keep_ref[:, columns] = product[:half]
    send_ref[:, columns] = product[half:].astype(jnp.bfloat16)


def part_kernel(bits, start, with_attention, *refs):
    if with_attention:
        place_ref, queries_ref, kv_ref, w_ref, *refs = refs
        *ahead_refs, context_ref, keep_ref, send_ref, buffer, arrived = refs
    else:
        context_ref, w_ref, *refs = refs
        *ahead_refs, keep_ref, send_ref, buffer, arrived = refs
    tiles = [(ref, index) for ref in ahead_refs for index in range(ref.shape[0])]
    missing = keep_ref.shape[1] // TILE - len(tiles)
    copies = fetches(start + len(tiles) * TILE, w_ref, buffer, arrived) if missing else []
    for copy in copies:
        copy.start()
    if with_attention:
        attend(bits, place_ref, queries_ref, kv_ref, context_ref)
    for index, (ref, tile) in enumerate(tiles):
        multiply(context_ref, ref[tile], index * TILE, keep_ref, send_ref)
    for index, copy in enumerate(copies):
        copy.wait()
        multiply(context_ref, buffer[index], (len(tiles) + index) * TILE, keep_ref, send_ref)


VMEM = pl.BlockSpec(memory_space=pltpu.VMEM)
SMEM = pl.BlockSpec(memory_space=pltpu.SMEM)
ANYWHERE = pl.BlockSpec(memory_space=pl.ANY)


def prepare(place, queries, bits):
    return pl.pallas_call(
        functools.partial(prepare_kernel, bits),
        in_specs=[SMEM, ANYWHERE],
        out_specs=VMEM,
        out_shape=jax.ShapeDtypeStruct(queries.shape, queries.dtype),
        scratch_shapes=[pltpu.VMEM(queries.shape, queries.dtype), pltpu.SemaphoreType.DMA],
        compiler_params=pltpu.CompilerParams(vmem_limit_bytes=LIMIT),
        cost_estimate=pl.CostEstimate(flops=0, bytes_accessed=4 * queries.size, transcendentals=0),
    )(place, queries)


def fetch(place, weight, start, tiles):
    return pl.pallas_call(
        functools.partial(fetch_kernel, start),
        in_specs=[SMEM, ANYWHERE],
        out_specs=VMEM,
        out_shape=jax.ShapeDtypeStruct((tiles, weight.shape[0], TILE), weight.dtype),
        scratch_shapes=[pltpu.SemaphoreType.DMA((tiles,))],
        compiler_params=pltpu.CompilerParams(vmem_limit_bytes=LIMIT),
    )(place, weight)


def project_part(bits, start, columns, context, first_inputs, weight, ahead):
    with_attention = context is None
    depth = weight.shape[0]
    total_rows = (first_inputs[1] if with_attention else context).shape[0]
    missing = max(columns // TILE - sum(array.shape[0] for array in ahead), 1)
    out_shape = [
        jax.ShapeDtypeStruct((total_rows // 2, columns), jnp.float32),
        jax.ShapeDtypeStruct((total_rows // 2, columns), jnp.bfloat16),
    ]
    inputs, in_specs = [context, weight], [VMEM, ANYWHERE]
    if with_attention:
        out_shape = [jax.ShapeDtypeStruct((total_rows, depth), jnp.bfloat16)] + out_shape
        inputs, in_specs = [*first_inputs, weight], [SMEM, VMEM, VMEM, ANYWHERE]
    return pl.pallas_call(
        functools.partial(part_kernel, bits, start, with_attention),
        in_specs=in_specs + [VMEM] * len(ahead),
        out_specs=[VMEM] * len(out_shape),
        out_shape=out_shape,
        scratch_shapes=[pltpu.VMEM((missing, depth, TILE), jnp.bfloat16), pltpu.SemaphoreType.DMA((missing,))],
        compiler_params=pltpu.CompilerParams(vmem_limit_bytes=LIMIT),
    )(*inputs, *ahead)


def finish_kernel(bounds, is_last, codes_ref, exponents_ref, *refs):
    i = lax.broadcasted_iota(jnp.int32, (HBLK, HBLK), 0)
    common = i & lax.broadcasted_iota(jnp.int32, (HBLK, HBLK), 1)
    parity = jnp.zeros((HBLK, HBLK), jnp.int32)
    for bit in range(HBLK.bit_length() - 1):
        parity = parity ^ (common >> bit)
    table = (1 - 2 * (parity & 1)).astype(jnp.bfloat16)
    scale = jnp.exp2(exponents_ref[...].astype(jnp.float32))
    if is_last:
        keep_ref, got_ref, *done_refs, out_ref = refs
        for start, done_ref in zip(bounds[1:], done_refs):
            out_ref[:, start:start + done_ref.shape[1]] = done_ref[...]
        jobs = [(bounds[0], keep_ref, got_ref, out_ref, bounds[0])]
    else:
        jobs = [(start, *refs[2 * n:2 * n + 2], refs[2 * len(bounds) + n], 0) for n, start in enumerate(bounds)]
    for start, keep_ref, got_ref, done_ref, at in jobs:
        rows, width = keep_ref.shape
        summed = keep_ref[...] + got_ref[...].astype(jnp.float32)
        blocks = width // HBLK
        rest = jnp.concatenate([summed[:, b * HBLK:(b + 1) * HBLK] for b in range(blocks)], axis=0)
        rotated = jnp.zeros_like(rest)
        for _ in range(3):
            piece = rest.astype(jnp.bfloat16)
            rotated = rotated + jnp.dot(piece, table, preferred_element_type=jnp.float32)
            rest = rest - piece.astype(jnp.float32)
        rotated = rotated * (1.0 / math.sqrt(HBLK))
        for b in range(blocks):
            block = start // HBLK + b
            codes = codes_ref[:, block * HBLK:(block + 1) * HBLK].astype(jnp.float32)
            done_ref[:, at + b * HBLK:at + (b + 1) * HBLK] = (
                codes * scale[:, block:block + 1] + rotated[b * rows:(b + 1) * rows]
            ).astype(jnp.bfloat16)


def finish(codes, exponents, pieces, bounds, done=None):
    is_last = done is not None
    rows, width = codes.shape
    shapes = [(rows, width)] if is_last else [keep.shape for keep in pieces[::2]]
    inputs = [codes, exponents, *pieces, *(done or [])]
    return pl.pallas_call(
        functools.partial(finish_kernel, bounds, is_last),
        in_specs=[VMEM] * len(inputs),
        out_specs=[VMEM] * len(shapes),
        out_shape=[jax.ShapeDtypeStruct(shape, jnp.bfloat16) for shape in shapes],
        compiler_params=pltpu.CompilerParams(vmem_limit_bytes=LIMIT),
    )(*inputs)


def passed_across(value, axis, mask):
    return lax.ppermute(value, axis, [(source, source ^ mask) for source in range(lax.axis_size(axis))])


def pack_kernel(local_heads, place_ref, rows_ref, packed_ref):
    query_group = QUERY_HEADS // KEY_VALUE_HEADS
    chip = place_ref[0] // 2
    for away in range(packed_ref.shape[0]):
        head = (chip ^ away) * 2 * local_heads // query_group
        columns = pl.ds(pl.multiple_of(head * HEAD_SIZE, HEAD_SIZE), HEAD_SIZE)
        for index in range(2):
            packed_ref[away, :, index * HEAD_SIZE:(index + 1) * HEAD_SIZE] = rows_ref[index, :, columns]


def shared_out(place, key_rows, value_rows, weight, bits, local_heads):
    rows = key_rows.shape[0]
    chips = 1 << (bits - 1)
    packed = pl.pallas_call(
        functools.partial(pack_kernel, local_heads),
        out_shape=jax.ShapeDtypeStruct((chips, rows, 2 * HEAD_SIZE), key_rows.dtype),
        in_specs=[SMEM, VMEM],
        out_specs=VMEM,
        compiler_params=pltpu.CompilerParams(vmem_limit_bytes=LIMIT),
    )(place, jnp.stack([key_rows, value_rows]))
    held = packed[:, None]
    ahead = []
    fetched = 0
    for bit in range(bits - 1):
        halves = held.reshape(-1, 2, *held.shape[1:])
        keep, send = halves[:, 0], halves[:, 1]
        got = passed_across(send, "tensor", 2 << bit)
        if bit < len(AHEAD):
            now, _ = lax.optimization_barrier((place, send))
            ahead.append(fetch(now, weight, fetched * TILE, AHEAD[bit]))
            fetched += AHEAD[bit]
            keep, got, ahead[-1] = lax.optimization_barrier((keep, got, ahead[-1]))
        held = jnp.concatenate([keep, got], axis=1)
    held = held[0]
    got = passed_across(held, "tensor", 1)
    return jnp.concatenate([held, got], axis=0).reshape(2 * chips * rows, 2 * HEAD_SIZE), ahead


def key_tokens(place_ref, bits, shape):
    index = lax.broadcasted_iota(jnp.int32, shape, 1)
    rows = shape[1] >> bits
    block = index // rows
    chips = 1 << (bits - 1)
    away = block // chips + 2 * (block % chips)
    return (place_ref[0] ^ away) * rows + index % rows


def body(encoded_query_rows, encoded_key_rows, head_value_rows, quant_codes, exponents, out_weight):
    total_rows, query_width = encoded_query_rows.shape
    depth, width = out_weight.shape
    devices = lax.axis_size("tensor")
    bits = devices.bit_length() - 1
    local_heads = query_width // HEAD_SIZE
    rows = total_rows // devices

    place = lax.axis_index("tensor").astype(jnp.int32).reshape(1)
    weight = pltpu.with_memory_space_constraint(out_weight, pltpu.HBM)
    queries = prepare(place, encoded_query_rows, bits)
    kv, ahead = shared_out(place, encoded_key_rows, head_value_rows, weight, bits, local_heads)
    unit = width // sum(columns for columns, *_ in PARTS)
    starts = [unit * sum(columns for columns, *_ in PARTS[:part]) for part in range(len(PARTS))]

    context = token = None
    state = {}
    fetched = {0: ahead}

    def summed_halves(part, step):
        nonlocal token
        left, keep, got = state.pop(part)
        keep, got, token = lax.optimization_barrier((keep, got, token))
        got = got[0] if len(got) == 1 else jnp.concatenate(got, axis=1)
        if step == bits:
            return left, keep, got
        columns = keep.shape[1]
        summed = (keep + got.astype(jnp.float32)).reshape((2,) * len(left) + (rows, columns))
        axis = left.index(halving_order(PARTS[part][1], bits)[step])
        keep, send = (lax.index_in_dim(summed, side, axis, keepdims=False).reshape(-1, columns) for side in (0, 1))
        return left[:axis] + left[axis + 1:], keep, send.astype(jnp.bfloat16)

    for part, step, *joined in events(bits):
        columns, order, tiles = PARTS[part]
        columns *= unit
        if step == -2:
            left, keep, got = state[part]
            early, token = lax.optimization_barrier((got[0], token))
            state[part] = left, keep, (early, *got[1:])
            continue
        if step == -1:
            now = place if token is None else lax.optimization_barrier((place, token))[0]
            token = fetch(now, weight, starts[part], tiles)
            fetched[part] = [token]
            continue
        if step == 0:
            if context is None:
                context, keep, send = project_part(bits, starts[part], columns, None, (place, queries, kv), weight, ahead)
            else:
                held, token = lax.optimization_barrier((context, token))
                keep, send = project_part(bits, starts[part], columns, held, None, weight, fetched.get(part, []))
            left = list(range(1, bits))
        else:
            left, keep, send = summed_halves(part, step)
            for other in joined:
                _, keep_too, send_too = summed_halves(other, step)
                keep = jnp.concatenate([keep, keep_too], axis=1)
                send = jnp.concatenate([send, send_too], axis=1)
        if step == bits:
            state[part], token = (left, keep, send), send
            continue
        cut = SPLIT.get(part, 0) * TILE if step == 1 else 0
        token = (send[:, :cut], send[:, cut:]) if cut else (send,)
        mask = 1 << halving_order(order, bits)[step]
        state[part] = left, keep, tuple(passed_across(piece, "tensor", mask) for piece in token)
    spare = max(8 - rows, 0)
    codes, scales = (jnp.pad(x, ((0, spare), (0, 0))) for x in (quant_codes, exponents))
    *early, last = [
        (starts[part], *(jnp.pad(x, ((0, spare), (0, 0))) for x in state[part][1:])) for part in state
    ]
    bounds = [start for start, _, _ in early]
    done = finish(codes, scales, [x for _, *pair in early for x in pair], bounds) if early else []
    (out,) = finish(codes, scales, last[1:], [last[0], *bounds], done)
    return out[:rows]


def solution(mesh):
    return jax.shard_map(
        body,
        mesh=mesh,
        in_specs=(
            P("groups", "tensor"),
            P(("groups", "tensor"), None),
            P(("groups", "tensor"), None),
            P(("groups", "tensor"), None),
            P(("groups", "tensor"), None),
            P("tensor", None),
        ),
        out_specs=P(("groups", "tensor"), None),
        check_vma=False,
    )
```

```python
import functools
import math

import jax
import jax.numpy as jnp
from jax import lax
from jax.experimental import pallas as pl
from jax.experimental.pallas import tpu as pltpu
from jax.sharding import PartitionSpec as P

QUERY_HEADS = 128
KEY_VALUE_HEADS = 8
HEAD_SIZE = 128
HBLK = 128
masked_score = -1e30

LIMIT = 12 << 20
PARTS = ((4, 'yz', 0), (4, 'yz', 0), (5, 'zyz', 3), (3, 'yz', 3))
AHEAD = (4, 4, 3)
TILE = 512
SPLIT = {}
EVENTS = ((0, 0), (2, -1), (0, 1), (1, 0), (2, 0), (0, 2), (1, 1), (2, 1), (3, -1), (3, 0), (1, 2), (3, 1), (0, 3), (2, 2), (1, 3), (3, 2), (2, 3), (0, 4), (1, 4), (3, 3), (2, 4), (3, 4))


def events(bits):
    if bits == 4:
        return EVENTS
    steps = range(-1, bits + 1)
    return [(part, step) for step in steps for part, (_, _, ahead) in enumerate(PARTS) if step >= 0 or (part and ahead)]


def halving_order(kind, bits):
    if kind == "yz":
        return list(range(bits))
    if kind == "zyz":
        return [0, 2, 1, *range(3, bits)]
    return [0, *range(2, bits), 1]


def reversed_bits(index, bits):
    result = 0
    for bit in range(bits):
        result = result + ((index >> bit) & 1) * (1 << (bits - 1 - bit))
    return result


def fetches(start, w_ref, buffer_ref, arrived):
    tiles, _, tile = buffer_ref.shape
    return [
        pltpu.make_async_copy(w_ref.at[:, pl.ds(start + index * tile, tile)], buffer_ref.at[index], arrived.at[index])
        for index in range(tiles)
    ]


def prepare_kernel(bits, place_ref, q_ref, queries_ref, held, arrived):
    copy = pltpu.make_async_copy(q_ref, held, arrived)
    copy.start()
    total_rows = q_ref.shape[0]
    column = lax.broadcasted_iota(jnp.int32, (total_rows, total_rows), 1)
    order = jnp.where(column == token_of_row(place_ref, total_rows, bits), 1.0, 0.0).astype(jnp.bfloat16)
    copy.wait()
    queries_ref[...] = jnp.dot(order, held[...], preferred_element_type=jnp.float32).astype(jnp.bfloat16)


def token_of_row(place_ref, total_rows, bits):
    rows = total_rows >> bits
    row = lax.broadcasted_iota(jnp.int32, (total_rows, 1), 0)
    return (place_ref[0] ^ reversed_bits(row // rows, bits)) * rows + row % rows


def attend(bits, place_ref, queries_ref, kv_ref, context_ref):
    total_rows = queries_ref.shape[0]
    visible = key_tokens(place_ref, bits, (total_rows, total_rows)) <= token_of_row(place_ref, total_rows, bits)
    key = kv_ref[:, :HEAD_SIZE]
    value = kv_ref[:, HEAD_SIZE:]
    for head in range(queries_ref.shape[1] // HEAD_SIZE):
        columns = slice(head * HEAD_SIZE, (head + 1) * HEAD_SIZE)
        scores = lax.dot_general(
            queries_ref[:, columns], key, (((1,), (1,)), ((), ())), preferred_element_type=jnp.float32
        ) * (1.0 / math.sqrt(HEAD_SIZE))
        scores = jnp.where(visible, scores, masked_score)
        top = jnp.max(scores, axis=1, keepdims=True)
        weights = jnp.where(visible, jnp.exp(scores - top), 0.0)
        total = jnp.sum(weights, axis=1, keepdims=True)
        high = weights.astype(jnp.bfloat16)
        low = (weights - high.astype(jnp.float32)).astype(jnp.bfloat16)
        weighted = jnp.dot(high, value, preferred_element_type=jnp.float32)
        weighted = weighted + jnp.dot(low, value, preferred_element_type=jnp.float32)
        context_ref[:, columns] = (weighted / total).astype(jnp.bfloat16)


def fetch_kernel(start, place_ref, w_ref, buffer_ref, arrived):
    copies = fetches(start, w_ref, buffer_ref, arrived)
    for copy in copies:
        copy.start()
    for copy in copies:
        copy.wait()


def multiply(context_ref, weight, at, keep_ref, send_ref):
    half = keep_ref.shape[0]
    columns = slice(at, at + weight.shape[1])
    product = jnp.dot(context_ref[...], weight, preferred_element_type=jnp.float32)
    keep_ref[:, columns] = product[:half]
    send_ref[:, columns] = product[half:].astype(jnp.bfloat16)


def part_kernel(bits, start, with_attention, ranges, *refs):
    if with_attention:
        place_ref, queries_ref, kv_ref, w_ref, *refs = refs
        *ahead_refs, context_ref, keep_ref, send_ref, buffer, arrived = refs
    else:
        context_ref, w_ref, *refs = refs
        *ahead_refs, keep_ref, send_ref, buffer, arrived = refs
    tiles = [(ref, index) for ref, (first, last) in zip(ahead_refs, ranges) for index in range(first, last)]
    missing = keep_ref.shape[1] // TILE - len(tiles)
    copies = fetches(start + len(tiles) * TILE, w_ref, buffer, arrived) if missing else []
    for copy in copies:
        copy.start()
    if with_attention:
        attend(bits, place_ref, queries_ref, kv_ref, context_ref)
    for index, (ref, tile) in enumerate(tiles):
        multiply(context_ref, ref[tile], index * TILE, keep_ref, send_ref)
    for index, copy in enumerate(copies):
        copy.wait()
        multiply(context_ref, buffer[index], (len(tiles) + index) * TILE, keep_ref, send_ref)


VMEM = pl.BlockSpec(memory_space=pltpu.VMEM)
SMEM = pl.BlockSpec(memory_space=pltpu.SMEM)
ANYWHERE = pl.BlockSpec(memory_space=pl.ANY)


def prepare(place, queries, bits):
    return pl.pallas_call(
        functools.partial(prepare_kernel, bits),
        in_specs=[SMEM, ANYWHERE],
        out_specs=VMEM,
        out_shape=jax.ShapeDtypeStruct(queries.shape, queries.dtype),
        scratch_shapes=[pltpu.VMEM(queries.shape, queries.dtype), pltpu.SemaphoreType.DMA],
        compiler_params=pltpu.CompilerParams(vmem_limit_bytes=LIMIT),
        cost_estimate=pl.CostEstimate(flops=0, bytes_accessed=4 * queries.size, transcendentals=0),
    )(place, queries)


def fetch(place, weight, start, tiles):
    return pl.pallas_call(
        functools.partial(fetch_kernel, start),
        in_specs=[SMEM, ANYWHERE],
        out_specs=VMEM,
        out_shape=jax.ShapeDtypeStruct((tiles, weight.shape[0], TILE), weight.dtype),
        scratch_shapes=[pltpu.SemaphoreType.DMA((tiles,))],
        compiler_params=pltpu.CompilerParams(vmem_limit_bytes=LIMIT),
    )(place, weight)


def project_part(bits, start, columns, context, first_inputs, weight, ahead):
    with_attention = context is None
    depth = weight.shape[0]
    total_rows = (first_inputs[1] if with_attention else context).shape[0]
    ranges = [(first, last) for _, first, last in ahead]
    missing = max(columns // TILE - sum(last - first for first, last in ranges), 1)
    out_shape = [
        jax.ShapeDtypeStruct((total_rows // 2, columns), jnp.float32),
        jax.ShapeDtypeStruct((total_rows // 2, columns), jnp.bfloat16),
    ]
    inputs, in_specs = [context, weight], [VMEM, ANYWHERE]
    if with_attention:
        out_shape = [jax.ShapeDtypeStruct((total_rows, depth), jnp.bfloat16)] + out_shape
        inputs, in_specs = [*first_inputs, weight], [SMEM, VMEM, VMEM, ANYWHERE]
    return pl.pallas_call(
        functools.partial(part_kernel, bits, start, with_attention, ranges),
        in_specs=in_specs + [VMEM] * len(ahead),
        out_specs=[VMEM] * len(out_shape),
        out_shape=out_shape,
        scratch_shapes=[pltpu.VMEM((missing, depth, TILE), jnp.bfloat16), pltpu.SemaphoreType.DMA((missing,))],
        compiler_params=pltpu.CompilerParams(vmem_limit_bytes=LIMIT),
    )(*inputs, *(array for array, _, _ in ahead))


def finish_kernel(bounds, is_last, codes_ref, exponents_ref, *refs):
    i = lax.broadcasted_iota(jnp.int32, (HBLK, HBLK), 0)
    common = i & lax.broadcasted_iota(jnp.int32, (HBLK, HBLK), 1)
    parity = jnp.zeros((HBLK, HBLK), jnp.int32)
    for bit in range(HBLK.bit_length() - 1):
        parity = parity ^ (common >> bit)
    table = (1 - 2 * (parity & 1)).astype(jnp.bfloat16)
    scale = jnp.exp2(exponents_ref[...].astype(jnp.float32))
    if is_last:
        keep_ref, got_ref, *done_refs, out_ref = refs
        for start, done_ref in zip(bounds[1:], done_refs):
            out_ref[:, start:start + done_ref.shape[1]] = done_ref[...]
        jobs = [(bounds[0], keep_ref, got_ref, out_ref, bounds[0])]
    else:
        jobs = [(start, *refs[2 * n:2 * n + 2], refs[2 * len(bounds) + n], 0) for n, start in enumerate(bounds)]
    for start, keep_ref, got_ref, done_ref, at in jobs:
        rows, width = keep_ref.shape
        summed = keep_ref[...] + got_ref[...].astype(jnp.float32)
        blocks = width // HBLK
        rest = jnp.concatenate([summed[:, b * HBLK:(b + 1) * HBLK] for b in range(blocks)], axis=0)
        rotated = jnp.zeros_like(rest)
        for _ in range(3):
            piece = rest.astype(jnp.bfloat16)
            rotated = rotated + jnp.dot(piece, table, preferred_element_type=jnp.float32)
            rest = rest - piece.astype(jnp.float32)
        rotated = rotated * (1.0 / math.sqrt(HBLK))
        for b in range(blocks):
            block = start // HBLK + b
            codes = codes_ref[:, block * HBLK:(block + 1) * HBLK].astype(jnp.float32)
            done_ref[:, at + b * HBLK:at + (b + 1) * HBLK] = (
                codes * scale[:, block:block + 1] + rotated[b * rows:(b + 1) * rows]
            ).astype(jnp.bfloat16)


def finish(codes, exponents, pieces, bounds, done=None):
    is_last = done is not None
    rows, width = codes.shape
    shapes = [(rows, width)] if is_last else [keep.shape for keep in pieces[::2]]
    inputs = [codes, exponents, *pieces, *(done or [])]
    return pl.pallas_call(
        functools.partial(finish_kernel, bounds, is_last),
        in_specs=[VMEM] * len(inputs),
        out_specs=[VMEM] * len(shapes),
        out_shape=[jax.ShapeDtypeStruct(shape, jnp.bfloat16) for shape in shapes],
        compiler_params=pltpu.CompilerParams(vmem_limit_bytes=LIMIT),
    )(*inputs)


def passed_across(value, axis, mask):
    return lax.ppermute(value, axis, [(source, source ^ mask) for source in range(lax.axis_size(axis))])


def pack_kernel(local_heads, place_ref, rows_ref, packed_ref):
    query_group = QUERY_HEADS // KEY_VALUE_HEADS
    chip = place_ref[0] // 2
    for away in range(packed_ref.shape[0]):
        head = (chip ^ away) * 2 * local_heads // query_group
        columns = pl.ds(pl.multiple_of(head * HEAD_SIZE, HEAD_SIZE), HEAD_SIZE)
        for index in range(2):
            packed_ref[away, :, index * HEAD_SIZE:(index + 1) * HEAD_SIZE] = rows_ref[index, :, columns]


def shared_out(place, key_rows, value_rows, weight, bits, local_heads):
    rows = key_rows.shape[0]
    chips = 1 << (bits - 1)
    packed = pl.pallas_call(
        functools.partial(pack_kernel, local_heads),
        out_shape=jax.ShapeDtypeStruct((chips, rows, 2 * HEAD_SIZE), key_rows.dtype),
        in_specs=[SMEM, VMEM],
        out_specs=VMEM,
        compiler_params=pltpu.CompilerParams(vmem_limit_bytes=LIMIT),
    )(place, jnp.stack([key_rows, value_rows]))
    held = packed[:, None]
    ahead = []
    fetched = 0
    for bit in range(bits - 1):
        halves = held.reshape(-1, 2, *held.shape[1:])
        keep, send = halves[:, 0], halves[:, 1]
        got = passed_across(send, "tensor", 2 << bit)
        if bit < len(AHEAD):
            now, _ = lax.optimization_barrier((place, send))
            ahead.append(fetch(now, weight, fetched * TILE, AHEAD[bit]))
            fetched += AHEAD[bit]
            keep, got, ahead[-1] = lax.optimization_barrier((keep, got, ahead[-1]))
        held = jnp.concatenate([keep, got], axis=1)
    held = held[0]
    got = passed_across(held, "tensor", 1)
    return jnp.concatenate([held, got], axis=0).reshape(2 * chips * rows, 2 * HEAD_SIZE), ahead


def key_tokens(place_ref, bits, shape):
    index = lax.broadcasted_iota(jnp.int32, shape, 1)
    rows = shape[1] >> bits
    block = index // rows
    chips = 1 << (bits - 1)
    away = block // chips + 2 * (block % chips)
    return (place_ref[0] ^ away) * rows + index % rows


def body(encoded_query_rows, encoded_key_rows, head_value_rows, quant_codes, exponents, out_weight):
    total_rows, query_width = encoded_query_rows.shape
    depth, width = out_weight.shape
    devices = lax.axis_size("tensor")
    bits = devices.bit_length() - 1
    local_heads = query_width // HEAD_SIZE
    rows = total_rows // devices

    place = lax.axis_index("tensor").astype(jnp.int32).reshape(1)
    weight = pltpu.with_memory_space_constraint(out_weight, pltpu.HBM)
    queries = prepare(place, encoded_query_rows, bits)
    kv, ahead = shared_out(place, encoded_key_rows, head_value_rows, weight, bits, local_heads)
    unit = width // sum(columns for columns, *_ in PARTS)
    starts = [unit * sum(columns for columns, *_ in PARTS[:part]) for part in range(len(PARTS))]

    context = token = None
    state = {}
    fetched = {}
    first = 0
    for array in ahead:
        for part, (columns, *_) in enumerate(PARTS):
            begin, end = starts[part] // TILE, (starts[part] + columns * unit) // TILE
            lowest, highest = max(begin, first), min(end, first + array.shape[0])
            if lowest < highest:
                fetched.setdefault(part, []).append((array, lowest - first, highest - first))
        first += array.shape[0]

    def summed_halves(part, step):
        nonlocal token
        left, keep, got = state.pop(part)
        keep, got, token = lax.optimization_barrier((keep, got, token))
        got = got[0] if len(got) == 1 else jnp.concatenate(got, axis=1)
        if step == bits:
            return left, keep, got
        columns = keep.shape[1]
        summed = (keep + got.astype(jnp.float32)).reshape((2,) * len(left) + (rows, columns))
        axis = left.index(halving_order(PARTS[part][1], bits)[step])
        keep, send = (lax.index_in_dim(summed, side, axis, keepdims=False).reshape(-1, columns) for side in (0, 1))
        return left[:axis] + left[axis + 1:], keep, send.astype(jnp.bfloat16)

    for part, step, *joined in events(bits):
        columns, order, tiles = PARTS[part]
        columns *= unit
        if step == -2:
            left, keep, got = state[part]
            early, token = lax.optimization_barrier((got[0], token))
            state[part] = left, keep, (early, *got[1:])
            continue
        if step == -1:
            now = place if token is None else lax.optimization_barrier((place, token))[0]
            token = fetch(now, weight, starts[part], tiles)
            fetched[part] = [(token, 0, tiles)]
            continue
        if step == 0:
            if context is None:
                context, keep, send = project_part(bits, starts[part], columns, None, (place, queries, kv), weight, fetched[0])
            else:
                held, token = lax.optimization_barrier((context, token))
                keep, send = project_part(bits, starts[part], columns, held, None, weight, fetched.get(part, []))
            left = list(range(1, bits))
        else:
            left, keep, send = summed_halves(part, step)
            for other in joined:
                _, keep_too, send_too = summed_halves(other, step)
                keep = jnp.concatenate([keep, keep_too], axis=1)
                send = jnp.concatenate([send, send_too], axis=1)
        if step == bits:
            state[part], token = (left, keep, send), send
            continue
        cut = SPLIT.get(part, 0) * TILE if step == 1 else 0
        token = (send[:, :cut], send[:, cut:]) if cut else (send,)
        mask = 1 << halving_order(order, bits)[step]
        state[part] = left, keep, tuple(passed_across(piece, "tensor", mask) for piece in token)
    spare = max(8 - rows, 0)
    codes, scales = (jnp.pad(x, ((0, spare), (0, 0))) for x in (quant_codes, exponents))
    *early, last = [
        (starts[part], *(jnp.pad(x, ((0, spare), (0, 0))) for x in state[part][1:])) for part in state
    ]
    bounds = [start for start, _, _ in early]
    done = finish(codes, scales, [x for _, *pair in early for x in pair], bounds) if early else []
    (out,) = finish(codes, scales, last[1:], [last[0], *bounds], done)
    return out[:rows]


def solution(mesh):
    return jax.shard_map(
        body,
        mesh=mesh,
        in_specs=(
            P("groups", "tensor"),
            P(("groups", "tensor"), None),
            P(("groups", "tensor"), None),
            P(("groups", "tensor"), None),
            P(("groups", "tensor"), None),
            P("tensor", None),
        ),
        out_specs=P(("groups", "tensor"), None),
        check_vma=False,
    )
```

```python
import functools
import math

import jax
import jax.numpy as jnp
from jax import lax
from jax.experimental import pallas as pl
from jax.experimental.pallas import tpu as pltpu
from jax.sharding import PartitionSpec as P

QUERY_HEADS = 128
KEY_VALUE_HEADS = 8
HEAD_SIZE = 128
HBLK = 128
masked_score = -1e30

LIMIT = 12 << 20
PARTS = ((4, 'yz', 0), (4, 'yz', 0), (5, 'zyz', 3), (3, 'yz', 3))
AHEAD = (4, 4, 3)
TILE = 512
SPLIT = {}
EVENTS = ((0, 0), (2, -1), (0, 1), (1, 0), (2, 0), (0, 2), (1, 1), (2, 1), (3, -1), (3, 0), (1, 2), (3, 1), (0, 3), (2, 2), (1, 3), (3, 2), (2, 3), (0, 4), (1, 4), (3, 3), (2, 4), (3, 4))


def events(bits):
    if bits == 4:
        return EVENTS
    steps = range(-1, bits + 1)
    return [(part, step) for step in steps for part, (_, _, ahead) in enumerate(PARTS) if step >= 0 or (part and ahead)]


def halving_order(kind, bits):
    if kind == "yz":
        return list(range(bits))
    if kind == "zyz":
        return [0, 2, 1, *range(3, bits)]
    return [0, *range(2, bits), 1]


def reversed_bits(index, bits):
    result = 0
    for bit in range(bits):
        result = result + ((index >> bit) & 1) * (1 << (bits - 1 - bit))
    return result


def fetches(start, w_ref, buffer_ref, arrived):
    tiles, _, tile = buffer_ref.shape
    return [
        pltpu.make_async_copy(w_ref.at[:, pl.ds(start + index * tile, tile)], buffer_ref.at[index], arrived.at[index])
        for index in range(tiles)
    ]


def prepare_kernel(bits, place_ref, q_ref, queries_ref, held, arrived):
    copy = pltpu.make_async_copy(q_ref, held, arrived)
    copy.start()
    total_rows = q_ref.shape[0]
    column = lax.broadcasted_iota(jnp.int32, (total_rows, total_rows), 1)
    order = jnp.where(column == token_of_row(place_ref, total_rows, bits), 1.0, 0.0).astype(jnp.bfloat16)
    copy.wait()
    queries_ref[...] = jnp.dot(order, held[...], preferred_element_type=jnp.float32).astype(jnp.bfloat16)


def token_of_row(place_ref, total_rows, bits):
    rows = total_rows >> bits
    row = lax.broadcasted_iota(jnp.int32, (total_rows, 1), 0)
    return (place_ref[0] ^ reversed_bits(row // rows, bits)) * rows + row % rows


def attend(bits, place_ref, queries_ref, kv_ref, context_ref):
    total_rows = queries_ref.shape[0]
    visible = key_tokens(place_ref, bits, (total_rows, total_rows)) <= token_of_row(place_ref, total_rows, bits)
    key = kv_ref[:, :HEAD_SIZE]
    value = kv_ref[:, HEAD_SIZE:]
    for head in range(queries_ref.shape[1] // HEAD_SIZE):
        columns = slice(head * HEAD_SIZE, (head + 1) * HEAD_SIZE)
        scores = lax.dot_general(
            queries_ref[:, columns], key, (((1,), (1,)), ((), ())), preferred_element_type=jnp.float32
        ) * (1.0 / math.sqrt(HEAD_SIZE))
        scores = jnp.where(visible, scores, masked_score)
        top = jnp.max(scores, axis=1, keepdims=True)
        weights = jnp.where(visible, jnp.exp(scores - top), 0.0)
        total = jnp.sum(weights, axis=1, keepdims=True)
        high = weights.astype(jnp.bfloat16)
        low = (weights - high.astype(jnp.float32)).astype(jnp.bfloat16)
        weighted = jnp.dot(high, value, preferred_element_type=jnp.float32)
        weighted = weighted + jnp.dot(low, value, preferred_element_type=jnp.float32)
        context_ref[:, columns] = (weighted / total).astype(jnp.bfloat16)


def fetch_kernel(start, place_ref, w_ref, buffer_ref, arrived):
    copies = fetches(start, w_ref, buffer_ref, arrived)
    for copy in copies:
        copy.start()
    for copy in copies:
        copy.wait()


def multiply(context_ref, weight, at, keep_ref, send_ref):
    half = keep_ref.shape[0]
    columns = slice(at, at + weight.shape[1])
    product = jnp.dot(context_ref[...], weight, preferred_element_type=jnp.float32)
    keep_ref[:, columns] = product[:half]
    send_ref[:, columns] = product[half:].astype(jnp.bfloat16)


def part_kernel(bits, start, with_attention, ranges, *refs):
    if with_attention:
        place_ref, queries_ref, kv_ref, w_ref, *refs = refs
        *ahead_refs, context_ref, keep_ref, send_ref, buffer, arrived = refs
    else:
        context_ref, w_ref, *refs = refs
        *ahead_refs, keep_ref, send_ref, buffer, arrived = refs
    tiles = [(ref, index) for ref, (first, last) in zip(ahead_refs, ranges) for index in range(first, last)]
    missing = keep_ref.shape[1] // TILE - len(tiles)
    copies = fetches(start + len(tiles) * TILE, w_ref, buffer, arrived) if missing else []
    for copy in copies:
        copy.start()
    if with_attention:
        attend(bits, place_ref, queries_ref, kv_ref, context_ref)
    for index, (ref, tile) in enumerate(tiles):
        multiply(context_ref, ref[tile], index * TILE, keep_ref, send_ref)
    for index, copy in enumerate(copies):
        copy.wait()
        multiply(context_ref, buffer[index], (len(tiles) + index) * TILE, keep_ref, send_ref)


VMEM = pl.BlockSpec(memory_space=pltpu.VMEM)
SMEM = pl.BlockSpec(memory_space=pltpu.SMEM)
ANYWHERE = pl.BlockSpec(memory_space=pl.ANY)


def prepare(place, queries, bits):
    return pl.pallas_call(
        functools.partial(prepare_kernel, bits),
        in_specs=[SMEM, ANYWHERE],
        out_specs=VMEM,
        out_shape=jax.ShapeDtypeStruct(queries.shape, queries.dtype),
        scratch_shapes=[pltpu.VMEM(queries.shape, queries.dtype), pltpu.SemaphoreType.DMA],
        compiler_params=pltpu.CompilerParams(vmem_limit_bytes=LIMIT),
        cost_estimate=pl.CostEstimate(flops=0, bytes_accessed=4 * queries.size, transcendentals=0),
    )(place, queries)


def fetch(place, weight, start, tiles):
    return pl.pallas_call(
        functools.partial(fetch_kernel, start),
        in_specs=[SMEM, ANYWHERE],
        out_specs=VMEM,
        out_shape=jax.ShapeDtypeStruct((tiles, weight.shape[0], TILE), weight.dtype),
        scratch_shapes=[pltpu.SemaphoreType.DMA((tiles,))],
        compiler_params=pltpu.CompilerParams(vmem_limit_bytes=LIMIT),
    )(place, weight)


def project_part(bits, start, columns, context, first_inputs, weight, ahead):
    with_attention = context is None
    depth = weight.shape[0]
    total_rows = (first_inputs[1] if with_attention else context).shape[0]
    ranges = [(first, last) for _, first, last in ahead]
    missing = max(columns // TILE - sum(last - first for first, last in ranges), 1)
    out_shape = [
        jax.ShapeDtypeStruct((total_rows // 2, columns), jnp.float32),
        jax.ShapeDtypeStruct((total_rows // 2, columns), jnp.bfloat16),
    ]
    inputs, in_specs = [context, weight], [VMEM, ANYWHERE]
    if with_attention:
        out_shape = [jax.ShapeDtypeStruct((total_rows, depth), jnp.bfloat16)] + out_shape
        inputs, in_specs = [*first_inputs, weight], [SMEM, VMEM, VMEM, ANYWHERE]
    return pl.pallas_call(
        functools.partial(part_kernel, bits, start, with_attention, ranges),
        in_specs=in_specs + [VMEM] * len(ahead),
        out_specs=[VMEM] * len(out_shape),
        out_shape=out_shape,
        scratch_shapes=[pltpu.VMEM((missing, depth, TILE), jnp.bfloat16), pltpu.SemaphoreType.DMA((missing,))],
        compiler_params=pltpu.CompilerParams(vmem_limit_bytes=LIMIT),
    )(*inputs, *(array for array, _, _ in ahead))


def finish_kernel(bounds, is_last, codes_ref, exponents_ref, *refs):
    i = lax.broadcasted_iota(jnp.int32, (HBLK, HBLK), 0)
    common = i & lax.broadcasted_iota(jnp.int32, (HBLK, HBLK), 1)
    parity = jnp.zeros((HBLK, HBLK), jnp.int32)
    for bit in range(HBLK.bit_length() - 1):
        parity = parity ^ (common >> bit)
    table = (1 - 2 * (parity & 1)).astype(jnp.bfloat16)
    scale = jnp.exp2(exponents_ref[...].astype(jnp.float32))
    if is_last:
        keep_ref, got_ref, *done_refs, out_ref = refs
        for start, done_ref in zip(bounds[1:], done_refs):
            out_ref[:, start:start + done_ref.shape[1]] = done_ref[...]
        jobs = [(bounds[0], keep_ref, got_ref, out_ref, bounds[0])]
    else:
        jobs = [(start, *refs[2 * n:2 * n + 2], refs[2 * len(bounds) + n], 0) for n, start in enumerate(bounds)]
    for start, keep_ref, got_ref, done_ref, at in jobs:
        rows, width = keep_ref.shape
        summed = keep_ref[...] + got_ref[...].astype(jnp.float32)
        blocks = width // HBLK
        rest = jnp.concatenate([summed[:, b * HBLK:(b + 1) * HBLK] for b in range(blocks)], axis=0)
        rotated = jnp.zeros_like(rest)
        for _ in range(2):
            piece = rest.astype(jnp.bfloat16)
            rotated = rotated + jnp.dot(piece, table, preferred_element_type=jnp.float32)
            rest = rest - piece.astype(jnp.float32)
        rotated = rotated * (1.0 / math.sqrt(HBLK))
        for b in range(blocks):
            block = start // HBLK + b
            codes = codes_ref[:, block * HBLK:(block + 1) * HBLK].astype(jnp.float32)
            done_ref[:, at + b * HBLK:at + (b + 1) * HBLK] = (
                codes * scale[:, block:block + 1] + rotated[b * rows:(b + 1) * rows]
            ).astype(jnp.bfloat16)


def finish(codes, exponents, pieces, bounds, done=None):
    is_last = done is not None
    rows, width = codes.shape
    shapes = [(rows, width)] if is_last else [keep.shape for keep in pieces[::2]]
    inputs = [codes, exponents, *pieces, *(done or [])]
    return pl.pallas_call(
        functools.partial(finish_kernel, bounds, is_last),
        in_specs=[VMEM] * len(inputs),
        out_specs=[VMEM] * len(shapes),
        out_shape=[jax.ShapeDtypeStruct(shape, jnp.bfloat16) for shape in shapes],
        compiler_params=pltpu.CompilerParams(vmem_limit_bytes=LIMIT),
    )(*inputs)


def passed_across(value, axis, mask):
    return lax.ppermute(value, axis, [(source, source ^ mask) for source in range(lax.axis_size(axis))])


def pack_kernel(local_heads, place_ref, rows_ref, packed_ref):
    query_group = QUERY_HEADS // KEY_VALUE_HEADS
    chip = place_ref[0] // 2
    for away in range(packed_ref.shape[0]):
        head = (chip ^ away) * 2 * local_heads // query_group
        columns = pl.ds(pl.multiple_of(head * HEAD_SIZE, HEAD_SIZE), HEAD_SIZE)
        for index in range(2):
            packed_ref[away, :, index * HEAD_SIZE:(index + 1) * HEAD_SIZE] = rows_ref[index, :, columns]


def shared_out(place, key_rows, value_rows, weight, bits, local_heads):
    rows = key_rows.shape[0]
    chips = 1 << (bits - 1)
    packed = pl.pallas_call(
        functools.partial(pack_kernel, local_heads),
        out_shape=jax.ShapeDtypeStruct((chips, rows, 2 * HEAD_SIZE), key_rows.dtype),
        in_specs=[SMEM, VMEM],
        out_specs=VMEM,
        compiler_params=pltpu.CompilerParams(vmem_limit_bytes=LIMIT),
    )(place, jnp.stack([key_rows, value_rows]))
    held = packed[:, None]
    ahead = []
    fetched = 0
    for bit in range(bits - 1):
        halves = held.reshape(-1, 2, *held.shape[1:])
        keep, send = halves[:, 0], halves[:, 1]
        got = passed_across(send, "tensor", 2 << bit)
        if bit < len(AHEAD):
            now, _ = lax.optimization_barrier((place, send))
            ahead.append(fetch(now, weight, fetched * TILE, AHEAD[bit]))
            fetched += AHEAD[bit]
            keep, got, ahead[-1] = lax.optimization_barrier((keep, got, ahead[-1]))
        held = jnp.concatenate([keep, got], axis=1)
    held = held[0]
    got = passed_across(held, "tensor", 1)
    return jnp.concatenate([held, got], axis=0).reshape(2 * chips * rows, 2 * HEAD_SIZE), ahead


def key_tokens(place_ref, bits, shape):
    index = lax.broadcasted_iota(jnp.int32, shape, 1)
    rows = shape[1] >> bits
    block = index // rows
    chips = 1 << (bits - 1)
    away = block // chips + 2 * (block % chips)
    return (place_ref[0] ^ away) * rows + index % rows


def body(encoded_query_rows, encoded_key_rows, head_value_rows, quant_codes, exponents, out_weight):
    total_rows, query_width = encoded_query_rows.shape
    depth, width = out_weight.shape
    devices = lax.axis_size("tensor")
    bits = devices.bit_length() - 1
    local_heads = query_width // HEAD_SIZE
    rows = total_rows // devices

    place = lax.axis_index("tensor").astype(jnp.int32).reshape(1)
    weight = pltpu.with_memory_space_constraint(out_weight, pltpu.HBM)
    queries = prepare(place, encoded_query_rows, bits)
    kv, ahead = shared_out(place, encoded_key_rows, head_value_rows, weight, bits, local_heads)
    unit = width // sum(columns for columns, *_ in PARTS)
    starts = [unit * sum(columns for columns, *_ in PARTS[:part]) for part in range(len(PARTS))]

    context = token = None
    state = {}
    fetched = {}
    first = 0
    for array in ahead:
        for part, (columns, *_) in enumerate(PARTS):
            begin, end = starts[part] // TILE, (starts[part] + columns * unit) // TILE
            lowest, highest = max(begin, first), min(end, first + array.shape[0])
            if lowest < highest:
                fetched.setdefault(part, []).append((array, lowest - first, highest - first))
        first += array.shape[0]

    def summed_halves(part, step):
        nonlocal token
        left, keep, got = state.pop(part)
        keep, got, token = lax.optimization_barrier((keep, got, token))
        got = got[0] if len(got) == 1 else jnp.concatenate(got, axis=1)
        if step == bits:
            return left, keep, got
        columns = keep.shape[1]
        summed = (keep + got.astype(jnp.float32)).reshape((2,) * len(left) + (rows, columns))
        axis = left.index(halving_order(PARTS[part][1], bits)[step])
        keep, send = (lax.index_in_dim(summed, side, axis, keepdims=False).reshape(-1, columns) for side in (0, 1))
        return left[:axis] + left[axis + 1:], keep, send.astype(jnp.bfloat16)

    for part, step, *joined in events(bits):
        columns, order, tiles = PARTS[part]
        columns *= unit
        if step == -2:
            left, keep, got = state[part]
            early, token = lax.optimization_barrier((got[0], token))
            state[part] = left, keep, (early, *got[1:])
            continue
        if step == -1:
            now = place if token is None else lax.optimization_barrier((place, token))[0]
            token = fetch(now, weight, starts[part], tiles)
            fetched[part] = [(token, 0, tiles)]
            continue
        if step == 0:
            if context is None:
                context, keep, send = project_part(bits, starts[part], columns, None, (place, queries, kv), weight, fetched[0])
            else:
                held, token = lax.optimization_barrier((context, token))
                keep, send = project_part(bits, starts[part], columns, held, None, weight, fetched.get(part, []))
            left = list(range(1, bits))
        else:
            left, keep, send = summed_halves(part, step)
            for other in joined:
                _, keep_too, send_too = summed_halves(other, step)
                keep = jnp.concatenate([keep, keep_too], axis=1)
                send = jnp.concatenate([send, send_too], axis=1)
        if step == bits:
            state[part], token = (left, keep, send), send
            continue
        cut = SPLIT.get(part, 0) * TILE if step == 1 else 0
        token = (send[:, :cut], send[:, cut:]) if cut else (send,)
        mask = 1 << halving_order(order, bits)[step]
        state[part] = left, keep, tuple(passed_across(piece, "tensor", mask) for piece in token)
    spare = max(8 - rows, 0)
    codes, scales = (jnp.pad(x, ((0, spare), (0, 0))) for x in (quant_codes, exponents))
    *early, last = [
        (starts[part], *(jnp.pad(x, ((0, spare), (0, 0))) for x in state[part][1:])) for part in state
    ]
    bounds = [start for start, _, _ in early]
    done = finish(codes, scales, [x for _, *pair in early for x in pair], bounds) if early else []
    (out,) = finish(codes, scales, last[1:], [last[0], *bounds], done)
    return out[:rows]


def solution(mesh):
    return jax.shard_map(
        body,
        mesh=mesh,
        in_specs=(
            P("groups", "tensor"),
            P(("groups", "tensor"), None),
            P(("groups", "tensor"), None),
            P(("groups", "tensor"), None),
            P(("groups", "tensor"), None),
            P("tensor", None),
        ),
        out_specs=P(("groups", "tensor"), None),
        check_vma=False,
    )
```
